256 devices in a mesh: seq: 32 (over z_hi, x, y), fsdp: 8 (over z_lo, core).
Axes of the slice: x: 4, y: 4, z: 8 (z_hi: 2, z_lo: 4; z = z_hi * 4 + z_lo), core: 2. Of those that a mesh axis runs over, the one named last changes fastest.
Arguments:
- latent: bfloat16 [8, 8192, 3584], P('fsdp', 'seq')
- targets: bfloat16 [8, 48, 96, 1536], P('fsdp', None, 'seq')
- index_map: int32 [8, 64, 128], P('fsdp'), may hold values from 0 to 4607, as said below
- proj_in: bfloat16 [3584, 1024], P(('seq', 'fsdp')), may hold values from -0.09375 to 0.09375
- proj_out: bfloat16 [1024, 1536], P(('seq', 'fsdp')), may hold values from -0.1875 to 0.1875
Outputs:
- grad_latent: bfloat16 [8, 8192, 3584], P('fsdp', 'seq')
- grad_in: float32 [3584, 1024], P(('seq', 'fsdp'))
- grad_out: float32 [1024, 1536], P(('seq', 'fsdp'))
The draws below stay inside these ranges and needn't reach their ends.
Inputs may be any that keep to these rules, and one draw needn't show every extreme that they name: index_map[b, i, j] = r_b(i) * 96 + c_b(j), one row function and one column function an image; c_b maps the latent columns k * 4 to (k + 1) * 4 - 1 into the target columns k * 3 to (k + 1) * 3 - 1 for every band k.
All inputs are finite; a program needn't handle non-finite values.
Results may differ from the reference program's by a relative error of at most 0.007.
Values may be sent and summed in bfloat16 or wider, within the bound.
No kernel may reach another device: no remote copies, remote signals or barrier semaphores. Data moves between devices by JAX's collectives and lax.ppermute only.
A program may use at most 128 MiB of HBM per device.

```python
import math
import jax
import jax.numpy as jnp
from jax import lax

D = 3584
PH = 1024
DT = 1536
W = 128
H = 64
S = 8192
TOK_DEV = 256
TW = 96
TH = 48
WC = 4
TC = 3
IMAGES = 8
N_SEQ = 32


def draw_latent(key, part):
    key = jax.random.fold_in(key, 3)
    first, second, third = jax.random.split(key, 3)
    feature_scale = jnp.exp(jax.random.uniform(third, (D,), jnp.float32, math.log(0.5), math.log(2.0)))
    row_scale = jnp.exp(jax.random.uniform(second, (IMAGES, S, 1), jnp.float32, math.log(0.3), math.log(3.0)))
    base = jax.random.normal(first, (IMAGES, S, D), jnp.float32)
    return (base * row_scale * feature_scale).astype(jnp.bfloat16)


def draw_targets(key, part):
    key = jax.random.fold_in(key, 5)
    first, second = jax.random.split(key, 2)
    row_scale = jnp.exp(jax.random.uniform(second, (IMAGES, TH, TW, 1), jnp.float32, 0.0, math.log(10.0)))
    base = jax.random.normal(first, (IMAGES, TH, TW, DT), jnp.float32)
    return (base * row_scale).astype(jnp.bfloat16)


def draw_index_map(key, part):
    key = jax.random.fold_in(key, 7)
    row_key, col_key = jax.random.split(key)
    rows = jnp.arange(H, dtype=jnp.int32)
    row_jitter = jax.random.randint(row_key, (IMAGES, H), -(H // 2), H // 2 + 1, jnp.int32)
    row_map = jnp.clip(((2 * rows + 1) * TH + row_jitter) // (2 * H), 0, TH - 1)
    cols = jnp.arange(W, dtype=jnp.int32)
    band = cols // WC
    inner = cols % WC
    col_jitter = jax.random.randint(col_key, (IMAGES, W), -WC, WC + 1, jnp.int32)
    col_map = band * TC + jnp.clip(((2 * inner + 1) * TC + col_jitter) // (2 * WC), 0, TC - 1)
    return (row_map[:, :, None] * TW + col_map[:, None, :]).astype(jnp.int32)


def block_levels(rng, extent, shards, smallest, high):
    def one(position, parts):
        heights = jax.random.uniform(jax.random.fold_in(jax.random.fold_in(rng, 6), position), (parts,), jnp.float32, smallest / len(shards), high / len(shards))
        return jnp.repeat(jnp.exp(heights), extent[position] // parts).reshape((-1,) + (1,) * (len(extent) - position - 1))

    loudness = one(*shards[0])
    for cut in shards[1:]:
        loudness = loudness * one(*cut)
    return loudness


def bell_draw(own_key, shape, width, reach, pieces=(), kind=jnp.bfloat16):
    level = block_levels(own_key, shape, pieces, -0.22, 0.18) if pieces else 1.0
    result = jax.random.normal(own_key, shape, jnp.float32) * width * level
    return jnp.minimum(jnp.maximum(result, -reach), reach).astype(kind)


def setup_inputs(seed: int = 0) -> dict:
    keys = jax.random.split(jax.random.key(seed), 6)
    latent = draw_latent(jax.random.fold_in(keys[5], 71), 0)
    targets = draw_targets(jax.random.fold_in(keys[5], 71), 0)
    index_map = draw_index_map(jax.random.fold_in(keys[5], 71), 0)
    proj_in = bell_draw(keys[3], (D, PH), D ** -0.5, 0.09375, ((0, 256),))
    proj_out = bell_draw(keys[4], (PH, DT), PH ** -0.5, 0.1875, ((0, 256),))
    return {"latent": latent, "targets": targets, "index_map": index_map, "proj_in": proj_in, "proj_out": proj_out}


loss_scale = 256.0
eps_norm = 1e-06

def silu_slope(pre):
    sig = jax.nn.sigmoid(pre)
    return sig * (1.0 + pre * (1.0 - sig))

def round_keep(value):
    rounded = lax.optimization_barrier(value.astype(jnp.bfloat16))
    return rounded.astype(jnp.float32)

def reference(latent, targets, index_map, proj_in, proj_out):
    block_count = IMAGES * N_SEQ
    rows = latent.reshape(block_count, TOK_DEV, D)
    maps = index_map.reshape(block_count, TOK_DEV).astype(jnp.int32)
    table = targets.reshape(IMAGES, TH * TW, DT)
    numbers = jnp.arange(block_count, dtype=jnp.int32)

    def step(carry, inputs):
        acc_in, acc_out = carry
        block, picks, number = inputs
        image = (number // N_SEQ).astype(jnp.int32)
        image_table = lax.dynamic_index_in_dim(table, image, 0, keepdims=False)
        goal = jnp.take(image_table, picks, axis=0).astype(jnp.float32)
        pre = jnp.dot(block, proj_in, preferred_element_type=jnp.float32)
        hidden = jax.nn.silu(pre).astype(jnp.bfloat16)
        pred = jnp.dot(hidden, proj_out, preferred_element_type=jnp.float32)
        norm_pred = jnp.sqrt(lax.optimization_barrier(jnp.sum(pred * pred, axis=1, keepdims=True)) + eps_norm)
        norm_goal = jnp.sqrt(lax.optimization_barrier(jnp.sum(goal * goal, axis=1, keepdims=True)) + eps_norm)
        cosv = lax.optimization_barrier(jnp.sum(pred * goal, axis=1, keepdims=True)) / (norm_pred * norm_goal)
        grad_pred = (-loss_scale * (goal / (norm_pred * norm_goal) - cosv * pred / (norm_pred * norm_pred))).astype(jnp.bfloat16)
        part_out = lax.dot_general(hidden, grad_pred, (((0,), (0,)), ((), ())), preferred_element_type=jnp.float32)
        grad_hidden = lax.dot_general(grad_pred, proj_out, (((1,), (1,)), ((), ())), preferred_element_type=jnp.float32)
        grad_pre = (grad_hidden * silu_slope(pre)).astype(jnp.bfloat16)
        part_in = lax.dot_general(block, grad_pre, (((0,), (0,)), ((), ())), preferred_element_type=jnp.float32)
        grad_block = lax.dot_general(grad_pre, proj_in, (((1,), (1,)), ((), ())), preferred_element_type=jnp.float32)
        return ((acc_in + round_keep(part_in), acc_out + round_keep(part_out)), grad_block.astype(jnp.bfloat16))
    start = (jnp.zeros((D, PH), jnp.float32), jnp.zeros((PH, DT), jnp.float32))
    (grad_in, grad_out), grads = lax.scan(step, start, (rows, maps, numbers))
    grad_latent = grads.reshape(IMAGES, S, D)
    return (grad_latent, grad_in, grad_out)
```

```python
import jax
import jax.numpy as jnp
import numpy as np
from jax import lax
from jax.experimental import pallas as pl
from jax.experimental.pallas import tpu as pltpu
from jax.sharding import Mesh, PartitionSpec as P

loss_scale = 256.0
eps_norm = 1e-06

AXES = ("zh", "x", "y", "zl", "c")
SIZES = (2, 4, 4, 4, 2)
D, PH, DT, TOK = 3584, 1024, 1536, 256
HH, HO = PH // 2, DT // 2
ROWS_IN, ROWS_OUT = 112, 32
PACK = 320
bf16, f32 = jnp.bfloat16, jnp.float32
NT = (((1,), (1,)), ((), ()))
TN = (((0,), (0,)), ((), ()))


def permute(v, move):
    pairs = []
    for i in range(256):
        here = [int(a) for a in np.unravel_index(i, SIZES)]
        there = [a % s for a, s in zip(move(*here), SIZES)]
        pairs.append((i, int(np.ravel_multi_index(there, SIZES))))
    return lax.ppermute(v, AXES, pairs)


def first_axis(v, d):
    return permute(
        v, lambda zh, x, y, zl, c: (zh, x + d * (c == 0), y + d * (c == 1), zl, c)
    )


def second_axis(v, d):
    return permute(
        v, lambda zh, x, y, zl, c: (zh, x + d * (c == 1), y + d * (c == 0), zl, c)
    )


def swap_cores(v):
    return permute(v, lambda zh, x, y, zl, c: (zh, x, y, zl, 1 - c))


def place_of(core, x, y, d3, d2):
    sx = lax.rem(x + jnp.where(core == 0, d2, d3), 4)
    sy = lax.rem(y + jnp.where(core == 0, d3, d2), 4)
    return sx, sy


SHIFTS = (0, 1, 3, 2)


def head_kernel(
    place,
    latent,
    picked,
    expand,
    *refs,
):
    own, oth = refs[0:4], refs[4:8]
    grad_pre_ref, grad_pred_ref, out_own, out_oth, w_in_out = refs[8:13]
    w_in, w_out, pre, hidden, pred, gpred, sems = refs[13:]
    x, y, c = place[0], place[1], place[2]

    def copies(half_refs, core, which):
        made = []
        for k, d3 in enumerate(SHIFTS):
            for j, d2 in enumerate(SHIFTS):
                sx, sy = place_of(core, x, y, 4 - d3, 4 - d2)
                src = half_refs[k].at[j]
                if which == "in":
                    for zh in range(2):
                        made.append(
                            pltpu.make_async_copy(
                                src.at[pl.ds(zh * ROWS_IN, ROWS_IN)],
                                w_in.at[
                                    zh * 16 + sx * 4 + sy,
                                    :,
                                    pl.ds(pl.multiple_of(core * HH, HH), HH),
                                ],
                                sems.at[0],
                            )
                        )
                else:
                    for zh in range(2):
                        rows = pl.ds(
                            pl.multiple_of((zh * 16 + sx * 4 + sy) * ROWS_OUT, ROWS_OUT),
                            ROWS_OUT,
                        )
                        made.append(
                            pltpu.make_async_copy(
                                src.at[pl.ds(224 + zh * 32, 32)],
                                w_out.at[
                                    rows, pl.ds(pl.multiple_of(core * HO, 256), 512)
                                ],
                                sems.at[1],
                            )
                        )
                        made.append(
                            pltpu.make_async_copy(
                                src.at[pl.ds(288, 32), pl.ds(zh * 256, 256)],
                                w_out.at[
                                    rows,
                                    pl.ds(pl.multiple_of(core * HO + 512, 256), 256),
                                ],
                                sems.at[1],
                            )
                        )
        return made

    first = copies(own, c, "in") + copies(oth, 1 - c, "in")
    second = copies(own, c, "out") + copies(oth, 1 - c, "out")
    for one in first:
        one.start()
    for one in second:
        one.start()
    goal = jnp.dot(expand[...], picked[...], preferred_element_type=f32)
    norm_goal = jnp.sqrt(jnp.sum(goal * goal, axis=1, keepdims=True) + eps_norm)
    pltpu.make_async_copy(w_in, w_in, sems.at[0]).wait()
    keep = pltpu.make_async_copy(w_in, w_in_out, sems.at[2])
    keep.start()
    lat = latent[...]
    for j in range(4):
        cols = slice(j * 256, (j + 1) * 256)
        part = jnp.dot(
            lat,
            w_in[:, :, cols].reshape(D, 256),
            preferred_element_type=f32,
        )
        pre[:, cols] = part
        hidden[:, cols] = (part * jax.nn.sigmoid(part)).astype(bf16)
    pltpu.make_async_copy(w_out, w_out, sems.at[1]).wait()
    for j in range(6):
        cols = slice(j * 256, (j + 1) * 256)
        pred[:, cols] = jnp.dot(hidden[...], w_out[:, cols], preferred_element_type=f32)
    guess = pred[...]
    norm_pred = jnp.sqrt(jnp.sum(guess * guess, axis=1, keepdims=True) + eps_norm)
    cosv = jnp.sum(guess * goal, axis=1, keepdims=True) / (norm_pred * norm_goal)
    grad_pred = (
        -loss_scale
        * (goal / (norm_pred * norm_goal) - cosv * guess / (norm_pred * norm_pred))
    ).astype(bf16)
    gpred[...] = grad_pred
    grad_pred_ref[...] = grad_pred
    for j in range(4):
        cols = slice(j * 256, (j + 1) * 256)
        grad_hidden = lax.dot_general(
            gpred[...], w_out[cols, :], NT, preferred_element_type=f32
        )
        part = pre[:, cols]
        sig = jax.nn.sigmoid(part)
        grad_pre_ref[:, cols] = (
            grad_hidden * (sig * (1.0 + part * (1.0 - sig)))
        ).astype(bf16)
    for ref, core in ((out_oth, 1 - c), (out_own, c)):
        for j in range(3):
            grads = gpred[:, pl.ds(pl.multiple_of(core * HO + j * 256, 256), 256)]
            ref[:, j * 256 : (j + 1) * 256] = lax.dot_general(
                hidden[...], grads, TN, preferred_element_type=f32
            ).astype(bf16)
    keep.wait()


def head(place, latent, picked, expand, own, oth):
    vmem = pl.BlockSpec(memory_space=pltpu.VMEM)
    hbm = pl.BlockSpec(memory_space=pl.ANY)
    return pl.pallas_call(
        head_kernel,
        in_specs=[pl.BlockSpec(memory_space=pltpu.SMEM)] + [vmem] * 3 + [hbm] * 8,
        out_specs=[vmem, vmem, vmem, vmem, hbm],
        out_shape=[
            jax.ShapeDtypeStruct((TOK, PH), bf16),
            jax.ShapeDtypeStruct((TOK, DT), bf16),
            jax.ShapeDtypeStruct((PH, HO), bf16),
            jax.ShapeDtypeStruct((PH, HO), bf16),
            jax.ShapeDtypeStruct((32, ROWS_IN, PH), bf16),
        ],
        scratch_shapes=[
            pltpu.VMEM((32, ROWS_IN, PH), bf16),
            pltpu.VMEM((PH, DT), bf16),
            pltpu.VMEM((TOK, PH), f32),
            pltpu.VMEM((TOK, PH), bf16),
            pltpu.VMEM((TOK, DT), f32),
            pltpu.VMEM((TOK, DT), bf16),
            pltpu.SemaphoreType.DMA((3,)),
        ],
        compiler_params=pltpu.CompilerParams(vmem_limit_bytes=48 * 2**20),
        cost_estimate=pl.CostEstimate(
            flops=6_000_000_000, bytes_accessed=30_000_000, transcendentals=600_000
        ),
        name="head",
    )(place, latent, picked, expand, *own, *oth)


def part_in_kernel(place, latent, grad_pre, own, oth):
    c = place[2]
    lat = latent[...]
    for ref, core in ((oth, 1 - c), (own, c)):
        grads = grad_pre[:, pl.ds(pl.multiple_of(core * HH, HH), HH)]
        ref[...] = lax.dot_general(lat, grads, TN, preferred_element_type=f32).astype(
            bf16
        )


def part_in(place, latent, grad_pre):
    step = 512
    block = pl.BlockSpec((step, HH), lambda i: (i, 0))
    return pl.pallas_call(
        part_in_kernel,
        grid=(D // step,),
        in_specs=[
            pl.BlockSpec(memory_space=pltpu.SMEM),
            pl.BlockSpec((TOK, step), lambda i: (0, i)),
            pl.BlockSpec((TOK, PH), lambda i: (0, 0)),
        ],
        out_specs=[block, block],
        out_shape=[jax.ShapeDtypeStruct((D, HH), bf16)] * 2,
        compiler_params=pltpu.CompilerParams(vmem_limit_bytes=32 * 2**20),
        cost_estimate=pl.CostEstimate(
            flops=1_900_000_000, bytes_accessed=10_000_000, transcendentals=0
        ),
        name="part_in",
    )(place, latent, grad_pre)


def back_kernel(grad_pre, w_in, out):
    out[...] = lax.dot_general(
        grad_pre[...], w_in[...], NT, preferred_element_type=f32
    ).astype(bf16)


def back(grad_pre, w_in):
    step = 512
    return pl.pallas_call(
        back_kernel,
        grid=(D // step,),
        in_specs=[
            pl.BlockSpec((TOK, PH), lambda i: (0, 0)),
            pl.BlockSpec((step, PH), lambda i: (i, 0)),
        ],
        out_specs=pl.BlockSpec((TOK, step), lambda i: (0, i)),
        out_shape=jax.ShapeDtypeStruct((TOK, D), bf16),
        compiler_params=pltpu.CompilerParams(vmem_limit_bytes=32 * 2**20),
        cost_estimate=pl.CostEstimate(
            flops=1_900_000_000, bytes_accessed=10_000_000, transcendentals=0
        ),
        name="back",
    )(grad_pre, w_in)


def pair_kernel(place, in_own, in_rcv, out_own, out_rcv, *outs):
    d3 = pl.program_id(0)
    top = (in_own[:, 0, 0].astype(f32) + in_rcv[:, 0, 0].astype(f32)).astype(bf16)
    low = (out_own[:, 0, 0].astype(f32) + out_rcv[:, 0, 0].astype(f32)).astype(bf16)
    for k in range(4):

        @pl.when(d3 == k)
        def _(k=k):
            out = outs[k]
            out[0, 0:112] = top[0]
            out[0, 112:224] = top[1]
            out[0, 224:256] = low[0, :, 0:512]
            out[0, 256:288] = low[1, :, 0:512]
            out[0, 288:320, 0:256] = low[0, :, 512:768]
            out[0, 288:320, 256:512] = low[1, :, 512:768]


def pair_sum(place, in_own, in_rcv, out_own, out_rcv):
    def spot(i, j, place):
        sx, sy = place_of(place[2], place[0], place[1], i, j)
        return (0, sx, sy, 0, 0)

    def slot(k):
        return lambda i, j, place: (jnp.where(i == k, j, jnp.where(i < k, 0, 3)), 0, 0)

    top = pl.BlockSpec((2, 1, 1, ROWS_IN, HH), spot)
    low = pl.BlockSpec((2, 1, 1, ROWS_OUT, HO), spot)
    shape_in, shape_out = (2, 4, 4, ROWS_IN, HH), (2, 4, 4, ROWS_OUT, HO)
    return pl.pallas_call(
        pair_kernel,
        grid_spec=pltpu.PrefetchScalarGridSpec(
            num_scalar_prefetch=1,
            grid=(4, 4),
            in_specs=[top, top, low, low],
            out_specs=[pl.BlockSpec((1, PACK, HH), slot(k)) for k in range(4)],
        ),
        out_shape=[jax.ShapeDtypeStruct((4, PACK, HH), bf16)] * 4,
        compiler_params=pltpu.CompilerParams(vmem_limit_bytes=32 * 2**20),
        cost_estimate=pl.CostEstimate(
            flops=6_000_000, bytes_accessed=16_000_000, transcendentals=0
        ),
        name="pair_sum",
    )(
        place,
        in_own.reshape(shape_in),
        in_rcv.reshape(shape_in),
        out_own.reshape(shape_out),
        out_rcv.reshape(shape_out),
    )


def add4(a, b, c, d):
    return (
        (a.astype(f32) + b.astype(f32)) + (c.astype(f32) + d.astype(f32))
    ).astype(bf16)


def per_device(latent, targets, index_map, proj_in, proj_out):
    x, y, c = lax.axis_index("x"), lax.axis_index("y"), lax.axis_index("c")
    place = jnp.stack([x, y, c]).astype(jnp.int32)

    halves = jnp.concatenate(
        [
            proj_in.reshape(14, 2, HH).transpose(1, 0, 2),
            proj_out.reshape(4, 2, HO).transpose(1, 0, 2).reshape(2, 6, HH),
        ],
        axis=1,
    )
    fan = jnp.broadcast_to(halves[None], (8, 2, 20, HH)).reshape(16, 20, HH)
    column = lax.all_to_all(
        fan, ("zh", "zl", "c"), split_axis=0, concat_axis=0, tiled=True
    )
    rows_in = column[:, :14].reshape(224, HH)
    rows_out = column[:, 14:].reshape(16, 4, HO).reshape(2, ROWS_OUT, HO)
    packed = jnp.concatenate(
        [
            rows_in,
            rows_out[:, :, :512].reshape(64, 512),
            rows_out[:, :, 512:].transpose(1, 0, 2).reshape(32, 512),
        ],
        axis=0,
    )
    line = jnp.stack([packed] + [first_axis(packed, d) for d in SHIFTS[1:]])
    own = [line] + [second_axis(line, d) for d in SHIFTS[1:]]
    oth = [swap_cores(v) for v in own]

    maps = index_map[0]
    width = targets.shape[2] * 32
    row_of = maps[:, 0] // width
    slab = targets[0].transpose(1, 0, 2)
    pick = (row_of[:, None] == jnp.arange(48, dtype=jnp.int32)[None]).astype(bf16)
    sent = jnp.stack(
        [jnp.dot(pick, slab[t], preferred_element_type=f32).astype(bf16) for t in range(3)]
    )
    sent, _ = lax.optimization_barrier((sent, line))
    got = lax.all_to_all(
        sent.reshape(3, 32, 2, DT).transpose(1, 0, 2, 3).reshape(32, 6, DT),
        ("zh", "x", "y"), split_axis=0, concat_axis=0, tiled=True,
    )
    picked = got.reshape(192, DT)
    col_of = (maps[0] % width).reshape(32, 4) - 3 * jnp.arange(32, dtype=jnp.int32)[:, None]
    token = jnp.arange(TOK, dtype=jnp.int32)[:, None]
    row = jnp.arange(192, dtype=jnp.int32)[None]
    want = ((token // 4) % 32) * 6 + jnp.tile(col_of.reshape(128), 2)[:, None] * 2 + token // 128
    expand = (row == want).astype(bf16)

    block = latent[0]
    grad_pre, grad_pred, out_own, out_oth, w_in = head(
        place, block, picked, expand, own, oth
    )
    in_own, in_oth = part_in(place, block, grad_pre)
    out_rcv = swap_cores(out_oth)
    in_rcv = swap_cores(in_oth)
    sums = pair_sum(place, in_own, in_rcv, out_own, out_rcv)
    got3 = [second_axis(sums[d], d) for d in SHIFTS[1:]]
    grad_latent = back(grad_pre, w_in.reshape(D, PH))
    line_sum = [add4(sums[0][k], got3[0][k], got3[1][k], got3[2][k]) for k in range(4)]
    got2 = [first_axis(line_sum[d], d) for d in SHIFTS[1:]]
    mine = add4(line_sum[0], *got2)
    g_in = mine[:224].reshape(16, 14, HH)
    g_out = jnp.concatenate(
        [
            mine[224:288].reshape(2, 32, 512),
            mine[288:].reshape(32, 2, 256).transpose(1, 0, 2),
        ],
        axis=2,
    ).reshape(16, 4, HO).reshape(16, 6, HH)
    last = lax.all_to_all(
        jnp.concatenate([g_in, g_out], axis=1),
        ("zh", "zl", "c"), split_axis=0, concat_axis=0, tiled=True,
    )
    total = jnp.sum(last.reshape(8, 2, 20, HH).astype(f32), axis=0)
    grad_in = total[:, :14].transpose(1, 0, 2).reshape(14, PH)
    grad_out = total[:, 14:].reshape(2, 4, HO).transpose(1, 0, 2).reshape(4, DT)
    return grad_latent[None], grad_in, grad_out


def solution(mesh):
    fine = Mesh(mesh.devices.reshape(SIZES), AXES)
    seq, fsdp = ("zh", "x", "y"), ("zl", "c")
    rows = P(AXES, None)
    return jax.shard_map(
        per_device,
        mesh=fine,
        in_specs=(P(fsdp, seq, None), P(fsdp, None, seq, None), P(fsdp, None, None), rows, rows),
        out_specs=(P(fsdp, seq, None), rows, rows),
        check_vma=False,
    )
```

```python
import jax
import jax.numpy as jnp
import numpy as np
from jax import lax
from jax.experimental import pallas as pl
from jax.experimental.pallas import tpu as pltpu
from jax.sharding import Mesh, PartitionSpec as P

loss_scale = 256.0
eps_norm = 1e-06

AXES = ("zh", "x", "y", "zl", "c")
SIZES = (2, 4, 4, 4, 2)
D, PH, DT, TOK = 3584, 1024, 1536, 256
HH, HO = PH // 2, DT // 2
ROWS_IN, ROWS_OUT = 112, 32
PACK = 320
HID = HH + HO
bf16, f32 = jnp.bfloat16, jnp.float32
NT = (((1,), (1,)), ((), ()))
TN = (((0,), (0,)), ((), ()))


def permute(v, move):
    pairs = []
    for i in range(256):
        here = [int(a) for a in np.unravel_index(i, SIZES)]
        there = [a % s for a, s in zip(move(*here), SIZES)]
        pairs.append((i, int(np.ravel_multi_index(there, SIZES))))
    return lax.ppermute(v, AXES, pairs)


def first_axis(v, d):
    return permute(
        v, lambda zh, x, y, zl, c: (zh, x + d * (c == 0), y + d * (c == 1), zl, c)
    )


def second_axis(v, d):
    return permute(
        v, lambda zh, x, y, zl, c: (zh, x + d * (c == 1), y + d * (c == 0), zl, c)
    )


def swap_cores(v):
    return permute(v, lambda zh, x, y, zl, c: (zh, x, y, zl, 1 - c))


def place_of(core, x, y, d3, d2):
    sx = lax.rem(x + jnp.where(core == 0, d2, d3), 4)
    sy = lax.rem(y + jnp.where(core == 0, d3, d2), 4)
    return sx, sy


SHIFTS = (0, 1, 3, 2)


def head_kernel(place, latent, picked, expand, *refs):
    own, oth = refs[0:4], refs[4:8]
    grad_pre_ref, keep_ref, give_ref, w_in_out = refs[8:12]
    w_in, w_out, pre, pred, gpred, sems = refs[12:]
    x, y, c = place[0], place[1], place[2]

    def fetch(half_refs, core, sem_in, sem_out):
        for k, d3 in enumerate(SHIFTS):
            for j, d2 in enumerate(SHIFTS):
                sx, sy = place_of(core, x, y, 4 - d3, 4 - d2)
                src = half_refs[k].at[j]
                for zh in range(2):
                    cols = pl.ds(pl.multiple_of(core * HH, HH), HH)
                    pltpu.make_async_copy(
                        src.at[pl.ds(zh * ROWS_IN, ROWS_IN)],
                        w_in.at[zh * 16 + sx * 4 + sy, :, cols],
                        sems.at[sem_in],
                    ).start()
                    rows = pl.ds(
                        pl.multiple_of((zh * 16 + sx * 4 + sy) * ROWS_OUT, ROWS_OUT),
                        ROWS_OUT,
                    )
                    pltpu.make_async_copy(
                        src.at[pl.ds(224 + zh * 32, 32)],
                        w_out.at[rows, pl.ds(pl.multiple_of(core * HO, 256), 512)],
                        sems.at[sem_out],
                    ).start()
                    pltpu.make_async_copy(
                        src.at[pl.ds(288, 32), pl.ds(zh * 256, 256)],
                        w_out.at[rows, pl.ds(pl.multiple_of(core * HO + 512, 256), 256)],
                        sems.at[sem_out],
                    ).start()

    fetch(own, c, 0, 2)
    fetch(oth, 1 - c, 1, 2)
    goal = jnp.dot(expand[...], picked[...], preferred_element_type=f32)
    norm_goal = jnp.sqrt(jnp.sum(goal * goal, axis=1, keepdims=True) + eps_norm)
    half = w_in.at[:, :, pl.ds(0, HH)]
    for core, sem in ((c, 0), (1 - c, 1)):
        pltpu.make_async_copy(half, half, sems.at[sem]).wait()
        for j in range(2):
            cols = pl.ds(pl.multiple_of(core * HH + j * 256, 256), 256)
            part = jnp.dot(
                latent[...],
                w_in[:, :, cols].reshape(D, 256),
                preferred_element_type=f32,
            )
            pre[:, cols] = part
            keep_ref[:, pl.ds(pl.multiple_of(HID + core * HH + j * 256, 256), 256)] = (
                part * jax.nn.sigmoid(part)
            ).astype(bf16)
    save = pltpu.make_async_copy(w_in, w_in_out, sems.at[3])
    save.start()
    pltpu.make_async_copy(w_out, w_out, sems.at[2]).wait()
    for j in range(6):
        cols = slice(j * 256, (j + 1) * 256)
        pred[:, cols] = jnp.dot(
            keep_ref[:, HID:], w_out[:, cols], preferred_element_type=f32
        )
    guess = pred[...]
    norm_pred = jnp.sqrt(jnp.sum(guess * guess, axis=1, keepdims=True) + eps_norm)
    cosv = jnp.sum(guess * goal, axis=1, keepdims=True) / (norm_pred * norm_goal)
    gpred[...] = (
        -loss_scale
        * (goal / (norm_pred * norm_goal) - cosv * guess / (norm_pred * norm_pred))
    ).astype(bf16)
    for j in range(4):
        cols = slice(j * 256, (j + 1) * 256)
        grad_hidden = lax.dot_general(
            gpred[...], w_out[cols, :], NT, preferred_element_type=f32
        )
        part = pre[:, cols]
        sig = jax.nn.sigmoid(part)
        grad_pre_ref[:, cols] = (
            grad_hidden * (sig * (1.0 + part * (1.0 - sig)))
        ).astype(bf16)
    for ref, core in ((keep_ref, c), (give_ref, 1 - c)):
        ref[:, :HH] = grad_pre_ref[:, pl.ds(pl.multiple_of(core * HH, HH), HH)]
        ref[:, HH:HID] = gpred[:, pl.ds(pl.multiple_of(core * HO, 256), HO)]
    give_ref[:, HID:] = keep_ref[:, HID:]
    save.wait()


def head(place, latent, picked, expand, own, oth):
    vmem = pl.BlockSpec(memory_space=pltpu.VMEM)
    hbm = pl.BlockSpec(memory_space=pl.ANY)
    return pl.pallas_call(
        head_kernel,
        in_specs=[pl.BlockSpec(memory_space=pltpu.SMEM)] + [vmem] * 3 + [hbm] * 8,
        out_specs=[vmem, vmem, vmem, hbm],
        out_shape=[
            jax.ShapeDtypeStruct((TOK, PH), bf16),
            jax.ShapeDtypeStruct((TOK, HID + PH), bf16),
            jax.ShapeDtypeStruct((TOK, HID + PH), bf16),
            jax.ShapeDtypeStruct((32, ROWS_IN, PH), bf16),
        ],
        scratch_shapes=[
            pltpu.VMEM((32, ROWS_IN, PH), bf16),
            pltpu.VMEM((PH, DT), bf16),
            pltpu.VMEM((TOK, PH), f32),
            pltpu.VMEM((TOK, DT), f32),
            pltpu.VMEM((TOK, DT), bf16),
            pltpu.SemaphoreType.DMA((4,)),
        ],
        compiler_params=pltpu.CompilerParams(vmem_limit_bytes=40 * 2**20),
        cost_estimate=pl.CostEstimate(
            flops=5_000_000_000, bytes_accessed=30_000_000, transcendentals=600_000
        ),
        name="head",
    )(place, latent, picked, expand, *own, *oth)


def tail_kernel(place, lat_ref, keep, rcv, *refs):
    outs = refs[:4]
    p_in, p_out, sems = refs[4:]
    x, y, c = place[0], place[1], place[2]
    gpred = jnp.concatenate([keep[:, HH:HID], rcv[:, HH:HID]], axis=0)
    for zh in range(2):
        hid = slice(HID + zh * HH, HID + (zh + 1) * HH)
        hidden = jnp.concatenate([keep[:, hid], rcv[:, hid]], axis=0)
        p_out[zh * HH : (zh + 1) * HH] = lax.dot_general(
            hidden, gpred, TN, preferred_element_type=f32
        ).astype(bf16)
    gpre = jnp.concatenate([keep[:, :HH], rcv[:, :HH]], axis=0)
    for sx in range(4):
        for zh in range(2):
            b = zh * 16 + sx * 4
            rows = slice(b * ROWS_IN, (b + 4) * ROWS_IN)
            p_in[rows] = jnp.dot(
                lat_ref[rows], gpre, preferred_element_type=f32
            ).astype(bf16)
        for sy in range(4):
            dx, dy = lax.rem(sx + 4 - x, 4), lax.rem(sy + 4 - y, 4)
            d2, d3 = jnp.where(c == 0, dx, dy), jnp.where(c == 0, dy, dx)
            for k in range(4):

                @pl.when(d3 == k)
                def _(sx=sx, sy=sy, d2=d2, k=k):
                    dst = outs[k].at[d2]
                    for zh in range(2):
                        b = zh * 16 + sx * 4 + sy
                        low = pl.ds(b * ROWS_OUT, ROWS_OUT)
                        pltpu.make_async_copy(
                            p_in.at[pl.ds(b * ROWS_IN, ROWS_IN)],
                            dst.at[pl.ds(zh * ROWS_IN, ROWS_IN)],
                            sems.at[0],
                        ).start()
                        pltpu.make_async_copy(
                            p_out.at[low, pl.ds(0, 512)],
                            dst.at[pl.ds(224 + zh * 32, 32)],
                            sems.at[1],
                        ).start()
                        pltpu.make_async_copy(
                            p_out.at[low, pl.ds(512, 256)],
                            dst.at[pl.ds(288, 32), pl.ds(zh * 256, 256)],
                            sems.at[1],
                        ).start()

    pltpu.make_async_copy(p_in, p_in, sems.at[0]).wait()
    pltpu.make_async_copy(p_out, p_out, sems.at[1]).wait()


def tail(place, lat_both, keep, rcv):
    vmem = pl.BlockSpec(memory_space=pltpu.VMEM)
    hbm = pl.BlockSpec(memory_space=pl.ANY)
    return pl.pallas_call(
        tail_kernel,
        in_specs=[pl.BlockSpec(memory_space=pltpu.SMEM)] + [vmem] * 3,
        out_specs=[hbm] * 4,
        out_shape=[jax.ShapeDtypeStruct((4, PACK, HH), bf16)] * 4,
        scratch_shapes=[
            pltpu.VMEM((D, HH), bf16),
            pltpu.VMEM((PH, HO), bf16),
            pltpu.SemaphoreType.DMA((2,)),
        ],
        compiler_params=pltpu.CompilerParams(vmem_limit_bytes=40 * 2**20),
        cost_estimate=pl.CostEstimate(
            flops=2_700_000_000, bytes_accessed=12_000_000, transcendentals=0
        ),
        name="tail",
    )(place, lat_both, keep, rcv)


def back_kernel(grad_pre, w_in, out):
    out[...] = lax.dot_general(
        grad_pre[...], w_in[...], NT, preferred_element_type=f32
    ).astype(bf16)


def back(grad_pre, w_in):
    step = 512
    return pl.pallas_call(
        back_kernel,
        grid=(D // step,),
        in_specs=[
            pl.BlockSpec((TOK, PH), lambda i: (0, 0)),
            pl.BlockSpec((step, PH), lambda i: (i, 0)),
        ],
        out_specs=pl.BlockSpec((TOK, step), lambda i: (0, i)),
        out_shape=jax.ShapeDtypeStruct((TOK, D), bf16),
        compiler_params=pltpu.CompilerParams(vmem_limit_bytes=60 * 2**20),
        cost_estimate=pl.CostEstimate(
            flops=1_900_000_000, bytes_accessed=10_000_000, transcendentals=0
        ),
        name="back",
    )(grad_pre, w_in)


def add4(a, b, c, d):
    return (
        (a.astype(f32) + b.astype(f32)) + (c.astype(f32) + d.astype(f32))
    ).astype(bf16)


def per_device(latent, targets, index_map, proj_in, proj_out):
    x, y, c = lax.axis_index("x"), lax.axis_index("y"), lax.axis_index("c")
    place = jnp.stack([x, y, c]).astype(jnp.int32)

    halves = jnp.concatenate(
        [
            proj_in.reshape(14, 2, HH).transpose(1, 0, 2),
            proj_out.reshape(4, 2, HO).transpose(1, 0, 2).reshape(2, 6, HH),
        ],
        axis=1,
    )
    fan = jnp.broadcast_to(halves[None], (8, 2, 20, HH)).reshape(16, 20, HH)
    column = lax.all_to_all(
        fan, ("zh", "zl", "c"), split_axis=0, concat_axis=0, tiled=True
    )
    rows_in = column[:, :14].reshape(224, HH)
    rows_out = column[:, 14:].reshape(16, 4, HO).reshape(2, ROWS_OUT, HO)
    packed = jnp.concatenate(
        [
            rows_in,
            rows_out[:, :, :512].reshape(64, 512),
            rows_out[:, :, 512:].transpose(1, 0, 2).reshape(32, 512),
        ],
        axis=0,
    )
    maps = index_map[0]
    width = targets.shape[2] * 32
    row_of = maps[:, 0] // width
    slab = targets[0].transpose(1, 0, 2)
    pick = (row_of[:, None] == jnp.arange(48, dtype=jnp.int32)[None]).astype(bf16)
    sent = jnp.stack(
        [jnp.dot(pick, slab[t], preferred_element_type=f32).astype(bf16) for t in range(3)]
    )
    sent = sent.reshape(3, 32, 2, DT).transpose(1, 0, 2, 3).reshape(32, 6, DT)
    lat_t = latent[0].T
    packed, sent, lat_t = lax.optimization_barrier((packed, sent, lat_t))
    got = lax.all_to_all(
        sent, ("zh", "x", "y"), split_axis=0, concat_axis=0, tiled=True
    )
    line = jnp.stack([packed] + [first_axis(packed, d) for d in SHIFTS[1:]])
    lat_both = jnp.concatenate([lat_t, swap_cores(lat_t)], axis=1)
    own = [line] + [second_axis(line, d) for d in SHIFTS[1:]]
    own[1], got, lat_both = lax.optimization_barrier((own[1], got, lat_both))
    oth = [swap_cores(v) for v in own]
    picked = got.reshape(192, DT)
    col_of = (maps[0] % width).reshape(32, 4) - 3 * jnp.arange(32, dtype=jnp.int32)[:, None]
    token = jnp.arange(TOK, dtype=jnp.int32)[:, None]
    row = jnp.arange(192, dtype=jnp.int32)[None]
    want = ((token // 4) % 32) * 6 + jnp.tile(col_of.reshape(128), 2)[:, None] * 2 + token // 128
    expand = (row == want).astype(bf16)

    grad_pre, keep, give, w_in = head(place, latent[0], picked, expand, own, oth)
    rcv = swap_cores(give)
    grad_latent = back(grad_pre, w_in.reshape(D, PH))
    rcv, grad_latent = lax.optimization_barrier((rcv, grad_latent))
    sums = tail(place, lat_both, keep, rcv)
    got3 = [second_axis(sums[d], d) for d in SHIFTS[1:]]
    line_sum = [add4(sums[0][k], got3[0][k], got3[1][k], got3[2][k]) for k in range(4)]
    got2 = [first_axis(line_sum[d], d) for d in SHIFTS[1:]]
    mine = add4(line_sum[0], *got2)
    g_in = mine[:224].reshape(16, 14, HH)
    g_out = jnp.concatenate(
        [
            mine[224:288].reshape(2, 32, 512),
            mine[288:].reshape(32, 2, 256).transpose(1, 0, 2),
        ],
        axis=2,
    ).reshape(16, 4, HO).reshape(16, 6, HH)
    last = lax.all_to_all(
        jnp.concatenate([g_in, g_out], axis=1),
        ("zh", "zl", "c"), split_axis=0, concat_axis=0, tiled=True,
    )
    total = jnp.sum(last.reshape(8, 2, 20, HH).astype(f32), axis=0)
    grad_in = total[:, :14].transpose(1, 0, 2).reshape(14, PH)
    grad_out = total[:, 14:].reshape(2, 4, HO).transpose(1, 0, 2).reshape(4, DT)
    return grad_latent[None], grad_in, grad_out


def solution(mesh):
    fine = Mesh(mesh.devices.reshape(SIZES), AXES)
    seq, fsdp = ("zh", "x", "y"), ("zl", "c")
    rows = P(AXES, None)
    return jax.shard_map(
        per_device,
        mesh=fine,
        in_specs=(P(fsdp, seq, None), P(fsdp, None, seq, None), P(fsdp, None, None), rows, rows),
        out_specs=(P(fsdp, seq, None), rows, rows),
        check_vma=False,
    )
```

```python
import jax
import jax.numpy as jnp
import numpy as np
from jax import lax
from jax.experimental import pallas as pl
from jax.experimental.pallas import tpu as pltpu
from jax.sharding import Mesh, PartitionSpec as P

loss_scale = 256.0
eps_norm = 1e-06

AXES = ("zh", "x", "y", "zl", "c")
SIZES = (2, 4, 4, 4, 2)
D, PH, DT, TOK = 3584, 1024, 1536, 256
HH, HO = PH // 2, DT // 2
ROWS_IN, ROWS_OUT = 112, 32
PACK = 320
HID = HH + HO
bf16, f32 = jnp.bfloat16, jnp.float32
NT = (((1,), (1,)), ((), ()))
TN = (((0,), (0,)), ((), ()))


def permute(v, move):
    pairs = []
    for i in range(256):
        here = [int(a) for a in np.unravel_index(i, SIZES)]
        there = [a % s for a, s in zip(move(*here), SIZES)]
        pairs.append((i, int(np.ravel_multi_index(there, SIZES))))
    return lax.ppermute(v, AXES, pairs)


def first_axis(v, d):
    return permute(
        v, lambda zh, x, y, zl, c: (zh, x + d * (c == 0), y + d * (c == 1), zl, c)
    )


def second_axis(v, d):
    return permute(
        v, lambda zh, x, y, zl, c: (zh, x + d * (c == 1), y + d * (c == 0), zl, c)
    )


def swap_cores(v):
    return permute(v, lambda zh, x, y, zl, c: (zh, x, y, zl, 1 - c))


def place_of(core, x, y, d3, d2):
    sx = lax.rem(x + jnp.where(core == 0, d2, d3), 4)
    sy = lax.rem(y + jnp.where(core == 0, d3, d2), 4)
    return sx, sy


SHIFTS = (0, 1, 3, 2)
PIECES = ((0, 0, 512), (1, 0, 256), (3, 256, 256), (1, 256, 256), (3, 0, 256), (2, 0, 256), (2, 256, 256))


def head_kernel(place, latent, picked, expand, *refs):
    own, oth = refs[0:7], refs[7:14]
    grad_pre_ref, keep_ref, give_ref, w_in_out = refs[14:18]
    w_in, w_out, pre, pred, gpred, sems = refs[18:]
    x, y, c = place[0], place[1], place[2]

    def fetch(pieces, core, sem_in, sem_out):
        for ref, (d3, left, wide) in zip(pieces, PIECES):
            for j, d2 in enumerate(SHIFTS):
                sx, sy = place_of(core, x, y, 4 - d3, 4 - d2)
                b = sx * 4 + sy
                src = ref.at[j]

                def bring(rows, cols, dst, sem):
                    pltpu.make_async_copy(src.at[rows, cols], dst, sems.at[sem]).start()

                def lane(first, start, size):
                    return pl.ds(pl.multiple_of(first + start, 256), size)

                every = pl.ds(0, wide)
                bring(
                    pl.ds(0, 224),
                    every,
                    w_in.at[b, :, lane(core * HH, left, wide)],
                    sem_in,
                )
                bring(
                    pl.ds(224, 64),
                    every,
                    w_out.at[b, :, lane(core * HO, left, wide)],
                    sem_out,
                )
                for at in range(0, wide, 256):
                    zh = (left + at) // 256
                    bring(
                        pl.ds(288, 32),
                        pl.ds(at, 256),
                        w_out.at[b, pl.ds(zh * 32, 32), lane(core * HO, 512, 256)],
                        sem_out,
                    )

    fetch(own, c, 0, 2)
    fetch(oth, 1 - c, 1, 2)
    goal = jnp.dot(expand[...], picked[...], preferred_element_type=f32)
    norm_goal = jnp.sqrt(jnp.sum(goal * goal, axis=1, keepdims=True) + eps_norm)
    half = w_in.at[:, :, pl.ds(0, HH)]
    for core, sem in ((c, 0), (1 - c, 1)):
        pltpu.make_async_copy(half, half, sems.at[sem]).wait()
        for j in range(2):
            cols = pl.ds(pl.multiple_of(core * HH + j * 256, 256), 256)
            part = jnp.zeros((TOK, 256), f32)
            for zh in range(2):
                part += jnp.dot(
                    latent[:, zh * 1792 : (zh + 1) * 1792],
                    w_in[:, zh * ROWS_IN : (zh + 1) * ROWS_IN, cols].reshape(1792, 256),
                    preferred_element_type=f32,
                )
            pre[:, cols] = part
            keep_ref[:, pl.ds(pl.multiple_of(HID + core * HH + j * 256, 256), 256)] = (
                part * jax.nn.sigmoid(part)
            ).astype(bf16)
    save = pltpu.make_async_copy(w_in, w_in_out, sems.at[3])
    save.start()
    pltpu.make_async_copy(w_out, w_out, sems.at[2]).wait()
    for j in range(6):
        cols = slice(j * 256, (j + 1) * 256)
        part = jnp.zeros((TOK, 256), f32)
        for zh in range(2):
            part += jnp.dot(
                keep_ref[:, HID + zh * HH : HID + (zh + 1) * HH],
                w_out[:, zh * 32 : (zh + 1) * 32, cols].reshape(HH, 256),
                preferred_element_type=f32,
            )
        pred[:, cols] = part
    guess = pred[...]
    norm_pred = jnp.sqrt(jnp.sum(guess * guess, axis=1, keepdims=True) + eps_norm)
    cosv = jnp.sum(guess * goal, axis=1, keepdims=True) / (norm_pred * norm_goal)
    gpred[...] = (
        -loss_scale
        * (goal / (norm_pred * norm_goal) - cosv * guess / (norm_pred * norm_pred))
    ).astype(bf16)
    for j in range(4):
        cols = slice(j * 256, (j + 1) * 256)
        zh, b = j // 2, j % 2 * 8
        grad_hidden = lax.dot_general(
            gpred[...],
            w_out[b : b + 8, zh * 32 : (zh + 1) * 32, :].reshape(256, DT),
            NT,
            preferred_element_type=f32,
        )
        part = pre[:, cols]
        sig = jax.nn.sigmoid(part)
        grad_pre_ref[:, cols] = (
            grad_hidden * (sig * (1.0 + part * (1.0 - sig)))
        ).astype(bf16)
    for ref, core in ((keep_ref, c), (give_ref, 1 - c)):
        ref[:, :HH] = grad_pre_ref[:, pl.ds(pl.multiple_of(core * HH, HH), HH)]
        ref[:, HH:HID] = gpred[:, pl.ds(pl.multiple_of(core * HO, 256), HO)]
    give_ref[:, HID:] = keep_ref[:, HID:]
    save.wait()


def head(place, latent, picked, expand, own, oth):
    vmem = pl.BlockSpec(memory_space=pltpu.VMEM)
    hbm = pl.BlockSpec(memory_space=pl.ANY)
    return pl.pallas_call(
        head_kernel,
        in_specs=[pl.BlockSpec(memory_space=pltpu.SMEM)] + [vmem] * 3 + [hbm] * 14,
        out_specs=[vmem, vmem, vmem, hbm],
        out_shape=[
            jax.ShapeDtypeStruct((TOK, PH), bf16),
            jax.ShapeDtypeStruct((TOK, HID + PH), bf16),
            jax.ShapeDtypeStruct((TOK, HID + PH), bf16),
            jax.ShapeDtypeStruct((16, 2 * ROWS_IN, PH), bf16),
        ],
        scratch_shapes=[
            pltpu.VMEM((16, 2 * ROWS_IN, PH), bf16),
            pltpu.VMEM((16, 2 * ROWS_OUT, DT), bf16),
            pltpu.VMEM((TOK, PH), f32),
            pltpu.VMEM((TOK, DT), f32),
            pltpu.VMEM((TOK, DT), bf16),
            pltpu.SemaphoreType.DMA((4,)),
        ],
        compiler_params=pltpu.CompilerParams(vmem_limit_bytes=40 * 2**20),
        cost_estimate=pl.CostEstimate(
            flops=5_000_000_000, bytes_accessed=30_000_000, transcendentals=600_000
        ),
        name="head",
    )(place, latent, picked, expand, *own, *oth)


def tail_kernel(place, lat_a, lat_b, keep, rcv, *refs):
    outs = refs[:8]
    p_in, p_out = refs[8:]
    x, y, c = place[0], place[1], place[2]
    gpred = jnp.concatenate([keep[:, HH:HID], rcv[:, HH:HID]], axis=0)
    for zh in range(2):
        hid = slice(HID + zh * HH, HID + (zh + 1) * HH)
        hidden = jnp.concatenate([keep[:, hid], rcv[:, hid]], axis=0)
        p_out[zh * HH : (zh + 1) * HH] = lax.dot_general(
            hidden, gpred, TN, preferred_element_type=f32
        ).astype(bf16)
    for t in range(8):
        rows = slice(t * 448, (t + 1) * 448)
        p_in[rows] = (
            jnp.dot(lat_a[rows], keep[:, :HH], preferred_element_type=f32)
            + jnp.dot(lat_b[rows], rcv[:, :HH], preferred_element_type=f32)
        ).astype(bf16)
    for d3 in range(4):
        for d2 in range(4):
            sx, sy = place_of(c, x, y, d3, d2)
            b = sx * 4 + sy
            for zh in range(2):
                top = pl.ds(pl.multiple_of((zh * 16 + b) * ROWS_IN, 16), ROWS_IN)
                low = pl.ds(pl.multiple_of((zh * 16 + b) * ROWS_OUT, 32), ROWS_OUT)
                for h in range(2):
                    out = outs[d3 * 2 + h]
                    cols = slice(h * 256, (h + 1) * 256)
                    out[d2, zh * ROWS_IN : (zh + 1) * ROWS_IN] = p_in[top, cols]
                    out[d2, 224 + zh * 32 : 256 + zh * 32] = p_out[low, cols]
                outs[d3 * 2 + zh][d2, 288:320] = p_out[low, 512:768]


def tail(place, lat_a, lat_b, keep, rcv):
    vmem = pl.BlockSpec(memory_space=pltpu.VMEM)
    return pl.pallas_call(
        tail_kernel,
        in_specs=[pl.BlockSpec(memory_space=pltpu.SMEM)] + [vmem] * 4,
        out_specs=[vmem] * 8,
        out_shape=[jax.ShapeDtypeStruct((4, PACK, 256), bf16)] * 8,
        scratch_shapes=[pltpu.VMEM((D, HH), bf16), pltpu.VMEM((PH, HO), bf16)],
        compiler_params=pltpu.CompilerParams(vmem_limit_bytes=40 * 2**20),
        cost_estimate=pl.CostEstimate(
            flops=2_700_000_000, bytes_accessed=12_000_000, transcendentals=0
        ),
        name="tail",
    )(place, lat_a, lat_b, keep, rcv)


def back_kernel(grad_pre, w_in, out):
    out[...] = lax.dot_general(
        grad_pre[...], w_in[...].reshape(896, PH), NT, preferred_element_type=f32
    ).astype(bf16)


def back(grad_pre, w_in):
    return pl.pallas_call(
        back_kernel,
        grid=(4,),
        in_specs=[
            pl.BlockSpec((TOK, PH), lambda i: (0, 0)),
            pl.BlockSpec((8, ROWS_IN, PH), lambda i: (i % 2, i // 2, 0)),
        ],
        out_specs=pl.BlockSpec((TOK, 896), lambda i: (0, i)),
        out_shape=jax.ShapeDtypeStruct((TOK, D), bf16),
        compiler_params=pltpu.CompilerParams(vmem_limit_bytes=32 * 2**20),
        cost_estimate=pl.CostEstimate(
            flops=1_900_000_000, bytes_accessed=10_000_000, transcendentals=0
        ),
        name="back",
    )(grad_pre, w_in)


def add(*terms):
    return sum(t.astype(f32) for t in terms).astype(bf16)


def per_device(latent, targets, index_map, proj_in, proj_out):
    x, y, c = lax.axis_index("x"), lax.axis_index("y"), lax.axis_index("c")
    place = jnp.stack([x, y, c]).astype(jnp.int32)

    halves = jnp.concatenate(
        [
            proj_in.reshape(14, 2, HH).transpose(1, 0, 2),
            proj_out.reshape(4, 2, HO).transpose(1, 0, 2).reshape(2, 6, HH),
        ],
        axis=1,
    )
    fan = jnp.broadcast_to(halves[None], (8, 2, 20, HH)).reshape(16, 20, HH)
    column = lax.all_to_all(
        fan, ("zh", "zl", "c"), split_axis=0, concat_axis=0, tiled=True
    )
    rows_in = column[:, :14].reshape(224, HH)
    rows_out = column[:, 14:].reshape(16, 4, HO).reshape(2, ROWS_OUT, HO)
    packed = jnp.concatenate(
        [
            rows_in,
            rows_out[:, :, :512].reshape(64, 512),
            rows_out[:, :, 512:].transpose(1, 0, 2).reshape(32, 512),
        ],
        axis=0,
    )
    maps = index_map[0]
    width = targets.shape[2] * 32
    row_of = maps[:, 0] // width
    slab = targets[0].transpose(1, 0, 2)
    pick = (row_of[:, None] == jnp.arange(48, dtype=jnp.int32)[None]).astype(bf16)
    sent = jnp.stack(
        [jnp.dot(pick, slab[t], preferred_element_type=f32).astype(bf16) for t in range(3)]
    )
    sent = sent.reshape(3, 32, 2, DT).transpose(1, 0, 2, 3).reshape(32, 6, DT)
    lat_t = latent[0].T
    packed, sent, lat_t = lax.optimization_barrier((packed, sent, lat_t))
    got = lax.all_to_all(
        sent, ("zh", "x", "y"), split_axis=0, concat_axis=0, tiled=True
    )
    picked = got.reshape(192, DT)
    line = jnp.stack([packed] + [first_axis(packed, d) for d in SHIFTS[1:]])
    lat_o = swap_cores(lat_t)
    left, right = lax.optimization_barrier((line[..., :256], line[..., 256:]))
    left1, right3 = second_axis(left, 1), second_axis(right, 3)
    right1, left3 = second_axis(right, 1), second_axis(left, 3)
    left2, right2 = second_axis(left1, 1), second_axis(right3, 3)
    col_of = (maps[0] % width).reshape(32, 4) - 3 * jnp.arange(32, dtype=jnp.int32)[:, None]
    token = jnp.arange(TOK, dtype=jnp.int32)[:, None]
    row = jnp.arange(192, dtype=jnp.int32)[None]
    want = ((token // 4) % 32) * 6 + jnp.tile(col_of.reshape(128), 2)[:, None] * 2 + token // 128
    expand = (row == want).astype(bf16)

    right2, picked, expand = lax.optimization_barrier((right2, picked, expand))
    own = [line, left1, right3, right1, left3, left2, right2]
    oth = [swap_cores(v) for v in own]

    grad_pre, keep, give, w_in = head(place, latent[0], picked, expand, own, oth)
    rcv = swap_cores(give)
    sums = tail(place, lat_t, lat_o, keep, rcv)
    lefts, rights = sums[0::2], sums[1::2]
    via_left, via_right = second_axis(lefts[2], 1), second_axis(rights[2], 3)
    rights1, lefts3 = second_axis(rights[1], 1), second_axis(lefts[3], 3)
    lefts1 = second_axis(add(lefts[1], via_left), 1)
    rights3 = second_axis(add(rights[3], via_right), 3)
    grad_latent = back(grad_pre, w_in)
    lefts1, grad_latent = lax.optimization_barrier((lefts1, grad_latent))
    line_sum = [
        jnp.concatenate(
            [
                add(lefts[0][k], lefts1[k], lefts3[k]),
                add(rights[0][k], rights1[k], rights3[k]),
            ],
            axis=1,
        )
        for k in range(4)
    ]
    got2 = [first_axis(line_sum[d], d) for d in SHIFTS[1:]]
    mine = add(line_sum[0], *got2)
    g_in = mine[:224].reshape(16, 14, HH)
    g_out = jnp.concatenate(
        [
            mine[224:288].reshape(2, 32, 512),
            mine[288:].reshape(32, 2, 256).transpose(1, 0, 2),
        ],
        axis=2,
    ).reshape(16, 4, HO).reshape(16, 6, HH)
    last = lax.all_to_all(
        jnp.concatenate([g_in, g_out], axis=1),
        ("zh", "zl", "c"), split_axis=0, concat_axis=0, tiled=True,
    )
    total = jnp.sum(last.reshape(8, 2, 20, HH).astype(f32), axis=0)
    grad_in = total[:, :14].transpose(1, 0, 2).reshape(14, PH)
    grad_out = total[:, 14:].reshape(2, 4, HO).transpose(1, 0, 2).reshape(4, DT)
    return grad_latent[None], grad_in, grad_out


def solution(mesh):
    fine = Mesh(mesh.devices.reshape(SIZES), AXES)
    seq, fsdp = ("zh", "x", "y"), ("zl", "c")
    rows = P(AXES, None)
    return jax.shard_map(
        per_device,
        mesh=fine,
        in_specs=(P(fsdp, seq, None), P(fsdp, None, seq, None), P(fsdp, None, None), rows, rows),
        out_specs=(P(fsdp, seq, None), rows, rows),
        check_vma=False,
    )
```

```python
import jax
import jax.numpy as jnp
import numpy as np
from jax import lax
from jax.experimental import pallas as pl
from jax.experimental.pallas import tpu as pltpu
from jax.sharding import Mesh, PartitionSpec as P

loss_scale = 256.0
eps_norm = 1e-06

AXES = ("zh", "x", "y", "zl", "c")
SIZES = (2, 4, 4, 4, 2)
D, PH, DT, TOK = 3584, 1024, 1536, 256
HH, HO = PH // 2, DT // 2
ROWS_IN, ROWS_OUT = 112, 32
PACK = 320
HID = HH + HO
bf16, f32 = jnp.bfloat16, jnp.float32
NT = (((1,), (1,)), ((), ()))
TN = (((0,), (0,)), ((), ()))


def permute(v, move):
    pairs = []
    for i in range(256):
        here = [int(a) for a in np.unravel_index(i, SIZES)]
        there = [a % s for a, s in zip(move(*here), SIZES)]
        pairs.append((i, int(np.ravel_multi_index(there, SIZES))))
    return lax.ppermute(v, AXES, pairs)


def first_axis(v, d):
    return permute(
        v, lambda zh, x, y, zl, c: (zh, x + d * (c == 0), y + d * (c == 1), zl, c)
    )


def second_axis(v, d):
    return permute(
        v, lambda zh, x, y, zl, c: (zh, x + d * (c == 1), y + d * (c == 0), zl, c)
    )


def swap_cores(v):
    return permute(v, lambda zh, x, y, zl, c: (zh, x, y, zl, 1 - c))


def place_of(core, x, y, d3, d2):
    sx = lax.rem(x + jnp.where(core == 0, d2, d3), 4)
    sy = lax.rem(y + jnp.where(core == 0, d3, d2), 4)
    return sx, sy


SHIFTS = (0, 1, 3, 2)
PIECES = ((0, 0, 512), (1, 0, 256), (3, 256, 256), (1, 256, 256), (3, 0, 256), (2, 0, 256), (2, 256, 256))


def head_kernel(place, latent, picked, *refs):
    own, oth = refs[0:7], refs[7:14]
    grad_pre_ref, keep_ref, give_ref, w_in_out = refs[14:18]
    w_in, w_out, pre, pred, gpred, sems = refs[18:]
    x, y, c = place[0], place[1], place[2]

    def fetch(pieces, core, top, sem):
        for ref, (d3, left, wide) in zip(pieces, PIECES):
            for j, d2 in enumerate(SHIFTS):
                sx, sy = place_of(core, x, y, 4 - d3, 4 - d2)
                b = sx * 4 + sy
                src = ref.at[j]

                def bring(first, rows, at, size, dst):
                    pltpu.make_async_copy(
                        src.at[pl.ds(first, rows), pl.ds(at, size)], dst, sems.at[sem]
                    ).start()

                def lane(first, size):
                    return pl.ds(pl.multiple_of(first, 256), size)

                if top:
                    bring(0, 224, 0, wide, w_in.at[b, :, lane(core * HH + left, wide)])
                else:
                    bring(
                        224, 64, 0, wide, w_out.at[b, :, lane(core * HO + left, wide)]
                    )
                    for at in range(0, wide, 256):
                        rows = pl.ds((left + at) // 8, 32)
                        dst = w_out.at[b, rows, lane(core * HO + 512, 256)]
                        bring(288, 32, at, 256, dst)

    fetch(own, c, True, 0)
    fetch(oth, 1 - c, True, 1)
    fetch(own, c, False, 2)
    fetch(oth, 1 - c, False, 2)
    token = lax.broadcasted_iota(jnp.int32, (TOK, TOK), 0)
    row = lax.broadcasted_iota(jnp.int32, (TOK, TOK), 1)
    want = (token // 4 % 32) * 8 + token // 128 * 4 + token % 4
    expand = jnp.where(row == want, 1.0, 0.0).astype(bf16)
    goal = jnp.dot(expand, picked[...], preferred_element_type=f32)
    norm_goal = jnp.sqrt(jnp.sum(goal * goal, axis=1, keepdims=True) + eps_norm)
    half = w_in.at[:, :, pl.ds(0, HH)]
    for core, sem in ((c, 0), (1 - c, 1)):
        pltpu.make_async_copy(half, half, sems.at[sem]).wait()
        for j in range(2):
            cols = pl.ds(pl.multiple_of(core * HH + j * 256, 256), 256)
            part = jnp.zeros((TOK, 256), f32)
            for zh in range(2):
                part += jnp.dot(
                    latent[:, zh * 1792 : (zh + 1) * 1792],
                    w_in[:, zh * ROWS_IN : (zh + 1) * ROWS_IN, cols].reshape(1792, 256),
                    preferred_element_type=f32,
                )
            pre[:, cols] = part
            keep_ref[:, pl.ds(pl.multiple_of(HID + core * HH + j * 256, 256), 256)] = (
                part * jax.nn.sigmoid(part)
            ).astype(bf16)
    save = pltpu.make_async_copy(w_in, w_in_out, sems.at[3])
    save.start()
    pltpu.make_async_copy(w_out, w_out, sems.at[2]).wait()
    for j in range(6):
        cols = slice(j * 256, (j + 1) * 256)
        part = jnp.zeros((TOK, 256), f32)
        for zh in range(2):
            part += jnp.dot(
                keep_ref[:, HID + zh * HH : HID + (zh + 1) * HH],
                w_out[:, zh * 32 : (zh + 1) * 32, cols].reshape(HH, 256),
                preferred_element_type=f32,
            )
        pred[:, cols] = part
    guess = pred[...]
    norm_pred = jnp.sqrt(jnp.sum(guess * guess, axis=1, keepdims=True) + eps_norm)
    cosv = jnp.sum(guess * goal, axis=1, keepdims=True) / (norm_pred * norm_goal)
    gpred[...] = (
        -loss_scale
        * (goal / (norm_pred * norm_goal) - cosv * guess / (norm_pred * norm_pred))
    ).astype(bf16)
    for j in range(4):
        cols = slice(j * 256, (j + 1) * 256)
        zh, b = j // 2, j % 2 * 8
        grad_hidden = lax.dot_general(
            gpred[...],
            w_out[b : b + 8, zh * 32 : (zh + 1) * 32, :].reshape(256, DT),
            NT,
            preferred_element_type=f32,
        )
        part = pre[:, cols]
        sig = jax.nn.sigmoid(part)
        grad_pre_ref[:, cols] = (
            grad_hidden * (sig * (1.0 + part * (1.0 - sig)))
        ).astype(bf16)
    for ref, core in ((keep_ref, c), (give_ref, 1 - c)):
        ref[:, :HH] = grad_pre_ref[:, pl.ds(pl.multiple_of(core * HH, HH), HH)]
        ref[:, HH:HID] = gpred[:, pl.ds(pl.multiple_of(core * HO, 256), HO)]
    give_ref[:, HID:] = keep_ref[:, HID:]
    save.wait()


def head(place, latent, picked, own, oth):
    vmem = pl.BlockSpec(memory_space=pltpu.VMEM)
    hbm = pl.BlockSpec(memory_space=pltpu.HBM)
    return pl.pallas_call(
        head_kernel,
        in_specs=[pl.BlockSpec(memory_space=pltpu.SMEM)] + [vmem] * 2 + [hbm] * 14,
        out_specs=[vmem, vmem, vmem, hbm],
        out_shape=[
            jax.ShapeDtypeStruct((TOK, PH), bf16),
            jax.ShapeDtypeStruct((TOK, HID + PH), bf16),
            jax.ShapeDtypeStruct((TOK, HID + PH), bf16),
            jax.ShapeDtypeStruct((16, 2 * ROWS_IN, PH), bf16),
        ],
        scratch_shapes=[
            pltpu.VMEM((16, 2 * ROWS_IN, PH), bf16),
            pltpu.VMEM((16, 2 * ROWS_OUT, DT), bf16),
            pltpu.VMEM((TOK, PH), f32),
            pltpu.VMEM((TOK, DT), f32),
            pltpu.VMEM((TOK, DT), bf16),
            pltpu.SemaphoreType.DMA((4,)),
        ],
        compiler_params=pltpu.CompilerParams(vmem_limit_bytes=40 * 2**20),
        cost_estimate=pl.CostEstimate(
            flops=5_000_000_000, bytes_accessed=30_000_000, transcendentals=600_000
        ),
        name="head",
    )(place, latent, picked, *own, *oth)


def tail_kernel(place, lat_a, lat_b, keep, rcv, *refs):
    outs = refs[:8]
    p_in, p_out = refs[8:]
    x, y, c = place[0], place[1], place[2]
    gpred = jnp.concatenate([keep[:, HH:HID], rcv[:, HH:HID]], axis=0)
    for zh in range(2):
        hid = slice(HID + zh * HH, HID + (zh + 1) * HH)
        hidden = jnp.concatenate([keep[:, hid], rcv[:, hid]], axis=0)
        p_out[zh * HH : (zh + 1) * HH] = lax.dot_general(
            hidden, gpred, TN, preferred_element_type=f32
        ).astype(bf16)
    for t in range(8):
        rows = slice(t * 448, (t + 1) * 448)
        p_in[rows] = (
            jnp.dot(lat_a[rows], keep[:, :HH], preferred_element_type=f32)
            + jnp.dot(lat_b[rows], rcv[:, :HH], preferred_element_type=f32)
        ).astype(bf16)
    for d3 in range(4):
        for d2 in range(4):
            sx, sy = place_of(c, x, y, d3, d2)
            b = sx * 4 + sy
            for zh in range(2):
                top = pl.ds(pl.multiple_of((zh * 16 + b) * ROWS_IN, 16), ROWS_IN)
                low = pl.ds(pl.multiple_of((zh * 16 + b) * ROWS_OUT, 32), ROWS_OUT)
                for h in range(2):
                    out = outs[d3 * 2 + h]
                    cols = slice(h * 256, (h + 1) * 256)
                    out[d2, zh * ROWS_IN : (zh + 1) * ROWS_IN] = p_in[top, cols]
                    out[d2, 224 + zh * 32 : 256 + zh * 32] = p_out[low, cols]
                outs[d3 * 2 + zh][d2, 288:320] = p_out[low, 512:768]


def tail(place, lat_a, lat_b, keep, rcv):
    vmem = pl.BlockSpec(memory_space=pltpu.VMEM)
    return pl.pallas_call(
        tail_kernel,
        in_specs=[pl.BlockSpec(memory_space=pltpu.SMEM)] + [vmem] * 4,
        out_specs=[vmem] * 8,
        out_shape=[jax.ShapeDtypeStruct((4, PACK, 256), bf16)] * 8,
        scratch_shapes=[pltpu.VMEM((D, HH), bf16), pltpu.VMEM((PH, HO), bf16)],
        compiler_params=pltpu.CompilerParams(vmem_limit_bytes=40 * 2**20),
        cost_estimate=pl.CostEstimate(
            flops=2_700_000_000, bytes_accessed=12_000_000, transcendentals=0
        ),
        name="tail",
    )(place, lat_a, lat_b, keep, rcv)


def back_kernel(grad_pre, w_in, out):
    out[...] = lax.dot_general(
        grad_pre[...], w_in[...].reshape(896, PH), NT, preferred_element_type=f32
    ).astype(bf16)


def back(grad_pre, w_in):
    return pl.pallas_call(
        back_kernel,
        grid=(4,),
        in_specs=[
            pl.BlockSpec((TOK, PH), lambda i: (0, 0)),
            pl.BlockSpec((8, ROWS_IN, PH), lambda i: (i % 2, i // 2, 0)),
        ],
        out_specs=pl.BlockSpec((TOK, 896), lambda i: (0, i)),
        out_shape=jax.ShapeDtypeStruct((TOK, D), bf16),
        compiler_params=pltpu.CompilerParams(vmem_limit_bytes=32 * 2**20),
        cost_estimate=pl.CostEstimate(
            flops=1_900_000_000, bytes_accessed=10_000_000, transcendentals=0
        ),
        name="back",
    )(grad_pre, w_in)


def add(*terms):
    return sum(t.astype(f32) for t in terms).astype(bf16)


def fan_kernel(top, low, out):
    for h in range(2):
        lows = low[:, h * HO : (h + 1) * HO].astype(f32)
        block = jnp.concatenate(
            [
                top[:, h * HH : (h + 1) * HH].astype(f32),
                lows[:, :512],
                jnp.concatenate([lows[0:2, 512:], lows[2:4, 512:]], axis=1),
            ],
            axis=0,
        ).astype(bf16)
        for z in range(8):
            out[z * 2 + h] = block


def fan_out(proj_in, proj_out):
    return pl.pallas_call(
        fan_kernel,
        out_shape=jax.ShapeDtypeStruct((16, 20, HH), bf16),
        name="fan_out",
    )(proj_in, proj_out)


def fan_in_kernel(last, top, low):
    for h in range(2):
        total = last[h].astype(f32)
        for z in range(1, 8):
            total += last[z * 2 + h].astype(f32)
        top[:, h * HH : (h + 1) * HH] = total[:14]
        low[:, h * HO : h * HO + 512] = total[14:18]
        low[0:2, h * HO + 512 : (h + 1) * HO] = total[18:20, :256]
        low[2:4, h * HO + 512 : (h + 1) * HO] = total[18:20, 256:]


def fan_in(last):
    return pl.pallas_call(
        fan_in_kernel,
        out_shape=[
            jax.ShapeDtypeStruct((14, PH), f32),
            jax.ShapeDtypeStruct((4, DT), f32),
        ],
        name="fan_in",
    )(last)


def per_device(latent, targets, index_map, proj_in, proj_out):
    x, y, c = lax.axis_index("x"), lax.axis_index("y"), lax.axis_index("c")
    place = jnp.stack([x, y, c]).astype(jnp.int32)

    column = lax.all_to_all(
        fan_out(proj_in, proj_out),
        ("zh", "zl", "c"), split_axis=0, concat_axis=0, tiled=True,
    )
    third = jnp.concatenate([column[:, 18:, :256], column[:, 18:, 256:]], axis=1)
    packed = jnp.concatenate(
        [
            column[:, :14].reshape(224, HH),
            column[:, 14:18].reshape(64, HH),
            third.reshape(2, 32, 256).transpose(1, 0, 2).reshape(32, HH),
        ],
        axis=0,
    )

    seq = lax.axis_index("zh") * 16 + x * 4 + y
    slab = targets[0].transpose(1, 0, 2)
    wide, tall = slab.shape[:2]
    cell = lax.dynamic_slice_in_dim(index_map[0], seq * 4, 4, 1)
    cell = (cell % (wide * 32) - seq * wide) * tall + cell // (wide * 32)
    pick = (
        cell.reshape(TOK)[:, None] == jnp.arange(wide * tall, dtype=jnp.int32)[None]
    ).astype(bf16)
    sent = jnp.dot(
        pick, slab.reshape(wide * tall, DT), preferred_element_type=f32
    ).astype(bf16).reshape(32, 8, DT)
    lat_t = latent[0].T
    packed, sent, lat_t = lax.optimization_barrier((packed, sent, lat_t))
    got = lax.all_to_all(
        sent, ("zh", "x", "y"), split_axis=0, concat_axis=0, tiled=True
    )
    picked = got.reshape(TOK, DT)
    line = jnp.stack([packed] + [first_axis(packed, d) for d in SHIFTS[1:]])
    lat_o = swap_cores(lat_t)
    left, right = lax.optimization_barrier((line[..., :256], line[..., 256:]))
    left1, right3 = second_axis(left, 1), second_axis(right, 3)
    right1, left3 = second_axis(right, 1), second_axis(left, 3)
    left2, right2 = second_axis(left1, 1), second_axis(right3, 3)
    right2, picked = lax.optimization_barrier((right2, picked))
    own = [line, left1, right3, right1, left3, left2, right2]
    oth = [swap_cores(v) for v in own]

    grad_pre, keep, give, w_in = head(place, latent[0], picked, own, oth)
    rcv = swap_cores(give)
    sums = tail(place, lat_t, lat_o, keep, rcv)
    lefts, rights = sums[0::2], sums[1::2]
    via_left, via_right = second_axis(lefts[2], 1), second_axis(rights[2], 3)
    rights1, lefts3 = second_axis(rights[1], 1), second_axis(lefts[3], 3)
    lefts1 = second_axis(add(lefts[1], via_left), 1)
    rights3 = second_axis(add(rights[3], via_right), 3)
    grad_latent = back(grad_pre, w_in)
    lefts1, grad_latent = lax.optimization_barrier((lefts1, grad_latent))
    line_sum = [
        jnp.concatenate(
            [
                add(lefts[0][k], lefts1[k], lefts3[k]),
                add(rights[0][k], rights1[k], rights3[k]),
            ],
            axis=1,
        )
        for k in range(4)
    ]
    got2 = [first_axis(line_sum[d], d) for d in SHIFTS[1:]]
    mine = add(line_sum[0], *got2)
    third = mine[288:].reshape(32, 2, 256).transpose(1, 0, 2).reshape(16, 4, 256)
    last = lax.all_to_all(
        jnp.concatenate(
            [
                mine[:224].reshape(16, 14, HH),
                mine[224:288].reshape(16, 4, HH),
                jnp.concatenate([third[:, :2], third[:, 2:]], axis=2),
            ],
            axis=1,
        ),
        ("zh", "zl", "c"), split_axis=0, concat_axis=0, tiled=True,
    )
    grad_in, grad_out = fan_in(last)
    return grad_latent[None], grad_in, grad_out


def solution(mesh):
    fine = Mesh(mesh.devices.reshape(SIZES), AXES)
    seq, fsdp = ("zh", "x", "y"), ("zl", "c")
    rows = P(AXES, None)
    return jax.shard_map(
        per_device,
        mesh=fine,
        in_specs=(P(fsdp, seq, None), P(fsdp, None, seq, None), P(fsdp, None, None), rows, rows),
        out_specs=(P(fsdp, seq, None), rows, rows),
        check_vma=False,
    )
```

```python
import jax
import jax.numpy as jnp
import numpy as np
from jax import lax
from jax.experimental import pallas as pl
from jax.experimental.pallas import tpu as pltpu
from jax.sharding import Mesh, PartitionSpec as P

loss_scale = 256.0
eps_norm = 1e-06

AXES = ("zh", "x", "y", "zl", "c")
SIZES = (2, 4, 4, 4, 2)
D, PH, DT, TOK = 3584, 1024, 1536, 256
HH, HO = PH // 2, DT // 2
ROWS_IN, ROWS_OUT = 112, 32
PACK = 320
HID = HH + HO
bf16, f32 = jnp.bfloat16, jnp.float32
NT = (((1,), (1,)), ((), ()))
TN = (((0,), (0,)), ((), ()))


def permute(v, move):
    pairs = []
    for i in range(256):
        here = [int(a) for a in np.unravel_index(i, SIZES)]
        there = [a % s for a, s in zip(move(*here), SIZES)]
        pairs.append((i, int(np.ravel_multi_index(there, SIZES))))
    return lax.ppermute(v, AXES, pairs)


def first_axis(v, d):
    return permute(
        v, lambda zh, x, y, zl, c: (zh, x + d * (c == 0), y + d * (c == 1), zl, c)
    )


def second_axis(v, d):
    return permute(
        v, lambda zh, x, y, zl, c: (zh, x + d * (c == 1), y + d * (c == 0), zl, c)
    )


def swap_cores(v):
    return permute(v, lambda zh, x, y, zl, c: (zh, x, y, zl, 1 - c))


def place_of(core, x, y, d3, d2):
    sx = lax.rem(x + jnp.where(core == 0, d2, d3), 4)
    sy = lax.rem(y + jnp.where(core == 0, d3, d2), 4)
    return sx, sy


SHIFTS = (0, 1, 3, 2)
PIECES = ((0, 0, 512), (1, 0, 256), (3, 256, 256), (1, 256, 256), (3, 0, 256), (2, 0, 256), (2, 256, 256))


def head_kernel(place, latent, picked, *refs):
    own, oth = refs[0:7], refs[7:14]
    grad_pre_ref, keep_ref, give_ref, w_in_out = refs[14:18]
    w_in, w_out, pre, pred, gpred, sems = refs[18:]
    x, y, c = place[0], place[1], place[2]

    def fetch(pieces, core, top, sem):
        for ref, (d3, left, wide) in zip(pieces, PIECES):
            for j, d2 in enumerate(SHIFTS):
                sx, sy = place_of(core, x, y, 4 - d3, 4 - d2)
                b = sx * 4 + sy
                src = ref.at[j]

                def bring(first, rows, at, size, dst):
                    pltpu.make_async_copy(
                        src.at[pl.ds(first, rows), pl.ds(at, size)], dst, sems.at[sem]
                    ).start()

                def lane(first, size):
                    return pl.ds(pl.multiple_of(first, 256), size)

                if top:
                    bring(0, 224, 0, wide, w_in.at[b, :, lane(core * HH + left, wide)])
                else:
                    bring(
                        224, 64, 0, wide, w_out.at[b, :, lane(core * HO + left, wide)]
                    )
                    for at in range(0, wide, 256):
                        rows = pl.ds((left + at) // 8, 32)
                        dst = w_out.at[b, rows, lane(core * HO + 512, 256)]
                        bring(288, 32, at, 256, dst)

    fetch(own, c, True, 0)
    fetch(oth, 1 - c, True, 1)
    fetch(own, c, False, 2)
    fetch(oth, 1 - c, False, 2)
    token = lax.broadcasted_iota(jnp.int32, (TOK, TOK), 0)
    row = lax.broadcasted_iota(jnp.int32, (TOK, TOK), 1)
    want = (token // 4 % 32) * 8 + token // 128 * 4 + token % 4
    expand = jnp.where(row == want, 1.0, 0.0).astype(bf16)
    goal = jnp.dot(expand, picked[...], preferred_element_type=f32)
    norm_goal = jnp.sqrt(jnp.sum(goal * goal, axis=1, keepdims=True) + eps_norm)
    half = w_in.at[:, :, pl.ds(0, HH)]
    for core, sem in ((c, 0), (1 - c, 1)):
        pltpu.make_async_copy(half, half, sems.at[sem]).wait()
        for j in range(2):
            cols = pl.ds(pl.multiple_of(core * HH + j * 256, 256), 256)
            part = jnp.zeros((TOK, 256), f32)
            for zh in range(2):
                part += jnp.dot(
                    latent[:, zh * 1792 : (zh + 1) * 1792],
                    w_in[:, zh * ROWS_IN : (zh + 1) * ROWS_IN, cols].reshape(1792, 256),
                    preferred_element_type=f32,
                )
            pre[:, cols] = part
            keep_ref[:, pl.ds(pl.multiple_of(HID + core * HH + j * 256, 256), 256)] = (
                part * jax.nn.sigmoid(part)
            ).astype(bf16)
    save = pltpu.make_async_copy(w_in, w_in_out, sems.at[3])
    save.start()
    pltpu.make_async_copy(w_out, w_out, sems.at[2]).wait()
    for j in range(6):
        cols = slice(j * 256, (j + 1) * 256)
        part = jnp.zeros((TOK, 256), f32)
        for zh in range(2):
            part += jnp.dot(
                keep_ref[:, HID + zh * HH : HID + (zh + 1) * HH],
                w_out[:, zh * 32 : (zh + 1) * 32, cols].reshape(HH, 256),
                preferred_element_type=f32,
            )
        pred[:, cols] = part
    guess = pred[...]
    norm_pred = jnp.sqrt(jnp.sum(guess * guess, axis=1, keepdims=True) + eps_norm)
    cosv = jnp.sum(guess * goal, axis=1, keepdims=True) / (norm_pred * norm_goal)
    gpred[...] = (
        -loss_scale
        * (goal / (norm_pred * norm_goal) - cosv * guess / (norm_pred * norm_pred))
    ).astype(bf16)
    for j in range(4):
        cols = slice(j * 256, (j + 1) * 256)
        zh, b = j // 2, j % 2 * 8
        grad_hidden = lax.dot_general(
            gpred[...],
            w_out[b : b + 8, zh * 32 : (zh + 1) * 32, :].reshape(256, DT),
            NT,
            preferred_element_type=f32,
        )
        part = pre[:, cols]
        sig = jax.nn.sigmoid(part)
        grad_pre_ref[:, cols] = (
            grad_hidden * (sig * (1.0 + part * (1.0 - sig)))
        ).astype(bf16)
    for ref, core in ((keep_ref, c), (give_ref, 1 - c)):
        ref[:, :HH] = grad_pre_ref[:, pl.ds(pl.multiple_of(core * HH, HH), HH)]
        ref[:, HH:HID] = gpred[:, pl.ds(pl.multiple_of(core * HO, 256), HO)]
    give_ref[:, HID:] = keep_ref[:, HID:]
    save.wait()


def head(place, latent, picked, own, oth):
    vmem = pl.BlockSpec(memory_space=pltpu.VMEM)
    hbm = pl.BlockSpec(memory_space=pltpu.HBM)
    return pl.pallas_call(
        head_kernel,
        in_specs=[pl.BlockSpec(memory_space=pltpu.SMEM)] + [vmem] * 2 + [hbm] * 14,
        out_specs=[vmem, vmem, vmem, hbm],
        out_shape=[
            jax.ShapeDtypeStruct((TOK, PH), bf16),
            jax.ShapeDtypeStruct((TOK, HID + PH), bf16),
            jax.ShapeDtypeStruct((TOK, HID + PH), bf16),
            jax.ShapeDtypeStruct((16, 2 * ROWS_IN, PH), bf16),
        ],
        scratch_shapes=[
            pltpu.VMEM((16, 2 * ROWS_IN, PH), bf16),
            pltpu.VMEM((16, 2 * ROWS_OUT, DT), bf16),
            pltpu.VMEM((TOK, PH), f32),
            pltpu.VMEM((TOK, DT), f32),
            pltpu.VMEM((TOK, DT), bf16),
            pltpu.SemaphoreType.DMA((4,)),
        ],
        compiler_params=pltpu.CompilerParams(vmem_limit_bytes=40 * 2**20),
        cost_estimate=pl.CostEstimate(
            flops=5_000_000_000, bytes_accessed=30_000_000, transcendentals=600_000
        ),
        name="head",
    )(place, latent, picked, *own, *oth)


def tail_kernel(place, lat_a, lat_b, keep, rcv, *refs):
    outs = refs[:8]
    p_in, p_out = refs[8:]
    x, y, c = place[0], place[1], place[2]
    gpred = jnp.concatenate([keep[:, HH:HID], rcv[:, HH:HID]], axis=0)
    for zh in range(2):
        hid = slice(HID + zh * HH, HID + (zh + 1) * HH)
        hidden = jnp.concatenate([keep[:, hid], rcv[:, hid]], axis=0)
        p_out[zh * HH : (zh + 1) * HH] = lax.dot_general(
            hidden, gpred, TN, preferred_element_type=f32
        ).astype(bf16)
    for t in range(8):
        rows = slice(t * 448, (t + 1) * 448)
        p_in[rows] = (
            jnp.dot(lat_a[rows], keep[:, :HH], preferred_element_type=f32)
            + jnp.dot(lat_b[rows], rcv[:, :HH], preferred_element_type=f32)
        ).astype(bf16)
    for d3 in range(4):
        for d2 in range(4):
            sx, sy = place_of(c, x, y, d3, d2)
            b = sx * 4 + sy
            for zh in range(2):
                top = pl.ds(pl.multiple_of((zh * 16 + b) * ROWS_IN, 16), ROWS_IN)
                low = pl.ds(pl.multiple_of((zh * 16 + b) * ROWS_OUT, 32), ROWS_OUT)
                for h in range(2):
                    out = outs[d3 * 2 + h]
                    cols = slice(h * 256, (h + 1) * 256)
                    out[d2, zh * ROWS_IN : (zh + 1) * ROWS_IN] = p_in[top, cols]
                    out[d2, 224 + zh * 32 : 256 + zh * 32] = p_out[low, cols]
                outs[d3 * 2 + zh][d2, 288:320] = p_out[low, 512:768]


def tail(place, lat_a, lat_b, keep, rcv):
    vmem = pl.BlockSpec(memory_space=pltpu.VMEM)
    return pl.pallas_call(
        tail_kernel,
        in_specs=[pl.BlockSpec(memory_space=pltpu.SMEM)] + [vmem] * 4,
        out_specs=[vmem] * 8,
        out_shape=[jax.ShapeDtypeStruct((4, PACK, 256), bf16)] * 8,
        scratch_shapes=[pltpu.VMEM((D, HH), bf16), pltpu.VMEM((PH, HO), bf16)],
        compiler_params=pltpu.CompilerParams(vmem_limit_bytes=40 * 2**20),
        cost_estimate=pl.CostEstimate(
            flops=2_700_000_000, bytes_accessed=12_000_000, transcendentals=0
        ),
        name="tail",
    )(place, lat_a, lat_b, keep, rcv)


def back_kernel(grad_pre, w_in, out):
    out[...] = lax.dot_general(
        grad_pre[...], w_in[...].reshape(896, PH), NT, preferred_element_type=f32
    ).astype(bf16)


def back(grad_pre, w_in):
    return pl.pallas_call(
        back_kernel,
        grid=(4,),
        in_specs=[
            pl.BlockSpec((TOK, PH), lambda i: (0, 0)),
            pl.BlockSpec((8, ROWS_IN, PH), lambda i: (i % 2, i // 2, 0)),
        ],
        out_specs=pl.BlockSpec((TOK, 896), lambda i: (0, i)),
        out_shape=jax.ShapeDtypeStruct((TOK, D), bf16),
        compiler_params=pltpu.CompilerParams(vmem_limit_bytes=32 * 2**20),
        cost_estimate=pl.CostEstimate(
            flops=1_900_000_000, bytes_accessed=10_000_000, transcendentals=0
        ),
        name="back",
    )(grad_pre, w_in)


def add(*terms):
    return sum(t.astype(f32) for t in terms).astype(bf16)


def fan_kernel(top, low, out):
    for h in range(2):
        lows = low[:, h * HO : (h + 1) * HO].astype(f32)
        block = jnp.concatenate(
            [
                top[:, h * HH : (h + 1) * HH].astype(f32),
                lows[:, :512],
                jnp.concatenate([lows[0:2, 512:], lows[2:4, 512:]], axis=1),
            ],
            axis=0,
        ).astype(bf16)
        for z in range(8):
            out[z * 2 + h] = block


def fan_out(proj_in, proj_out):
    return pl.pallas_call(
        fan_kernel,
        out_shape=jax.ShapeDtypeStruct((16, 20, HH), bf16),
        name="fan_out",
    )(proj_in, proj_out)


def fan_in_kernel(last, top, low):
    for h in range(2):
        total = last[h].astype(f32)
        for z in range(1, 8):
            total += last[z * 2 + h].astype(f32)
        top[:, h * HH : (h + 1) * HH] = total[:14]
        low[:, h * HO : h * HO + 512] = total[14:18]
        low[0:2, h * HO + 512 : (h + 1) * HO] = total[18:20, :256]
        low[2:4, h * HO + 512 : (h + 1) * HO] = total[18:20, 256:]


def fan_in(last):
    return pl.pallas_call(
        fan_in_kernel,
        out_shape=[
            jax.ShapeDtypeStruct((14, PH), f32),
            jax.ShapeDtypeStruct((4, DT), f32),
        ],
        name="fan_in",
    )(last)


def per_device(latent, targets, index_map, proj_in, proj_out):
    x, y, c = lax.axis_index("x"), lax.axis_index("y"), lax.axis_index("c")
    place = jnp.stack([x, y, c]).astype(jnp.int32)

    column = lax.all_to_all(
        fan_out(proj_in, proj_out),
        ("zh", "zl", "c"), split_axis=0, concat_axis=0, tiled=True,
    )
    third = jnp.concatenate([column[:, 18:, :256], column[:, 18:, 256:]], axis=1)
    packed = jnp.concatenate(
        [
            column[:, :14].reshape(224, HH),
            column[:, 14:18].reshape(64, HH),
            third.reshape(2, 32, 256).transpose(1, 0, 2).reshape(32, HH),
        ],
        axis=0,
    )

    seq = lax.axis_index("zh") * 16 + x * 4 + y
    slab = targets[0].transpose(1, 0, 2)
    wide, tall = slab.shape[:2]
    cell = lax.dynamic_slice_in_dim(index_map[0], seq * 4, 4, 1)
    cell = (cell % (wide * 32) - seq * wide) * tall + cell // (wide * 32)
    pick = (
        cell.reshape(TOK)[:, None] == jnp.arange(wide * tall, dtype=jnp.int32)[None]
    ).astype(bf16)
    sent = jnp.dot(
        pick, slab.reshape(wide * tall, DT), preferred_element_type=f32
    ).astype(bf16).reshape(32, 8, DT)
    lat_t = latent[0].T
    packed, sent, lat_t = lax.optimization_barrier((packed, sent, lat_t))
    got = lax.all_to_all(
        sent, ("zh", "x", "y"), split_axis=0, concat_axis=0, tiled=True
    )
    picked = got.reshape(TOK, DT)
    line = jnp.stack([packed] + [first_axis(packed, d) for d in SHIFTS[1:]])
    lat_o = swap_cores(lat_t)
    left, right = lax.optimization_barrier((line[..., :256], line[..., 256:]))
    left1, right3 = second_axis(left, 1), second_axis(right, 3)
    right1, left3 = second_axis(right, 1), second_axis(left, 3)
    left2, right2 = second_axis(left1, 1), second_axis(right3, 3)
    right2, left2, picked = lax.optimization_barrier((right2, left2, picked))
    own = [line, left1, right3, right1, left3, left2, right2]
    oth = [swap_cores(v) for v in own]

    grad_pre, keep, give, w_in = head(place, latent[0], picked, own, oth)
    rcv = swap_cores(give)
    sums = tail(place, lat_t, lat_o, keep, rcv)
    lefts, rights = sums[0::2], sums[1::2]
    via_left, via_right = second_axis(lefts[2], 1), second_axis(rights[2], 3)
    rights1, lefts3 = second_axis(rights[1], 1), second_axis(lefts[3], 3)
    lefts1 = second_axis(add(lefts[1], via_left), 1)
    rights3 = second_axis(add(rights[3], via_right), 3)
    grad_latent = back(grad_pre, w_in)
    lefts1, grad_latent = lax.optimization_barrier((lefts1, grad_latent))
    line_sum = [
        jnp.concatenate(
            [
                add(lefts[0][k], lefts1[k], lefts3[k]),
                add(rights[0][k], rights1[k], rights3[k]),
            ],
            axis=1,
        )
        for k in range(4)
    ]
    got2 = [first_axis(line_sum[d], d) for d in SHIFTS[1:]]
    mine = add(line_sum[0], *got2)
    third = mine[288:].reshape(32, 2, 256).transpose(1, 0, 2).reshape(16, 4, 256)
    last = lax.all_to_all(
        jnp.concatenate(
            [
                mine[:224].reshape(16, 14, HH),
                mine[224:288].reshape(16, 4, HH),
                jnp.concatenate([third[:, :2], third[:, 2:]], axis=2),
            ],
            axis=1,
        ),
        ("zh", "zl", "c"), split_axis=0, concat_axis=0, tiled=True,
    )
    grad_in, grad_out = fan_in(last)
    return grad_latent[None], grad_in, grad_out


def solution(mesh):
    fine = Mesh(mesh.devices.reshape(SIZES), AXES)
    seq, fsdp = ("zh", "x", "y"), ("zl", "c")
    rows = P(AXES, None)
    return jax.shard_map(
        per_device,
        mesh=fine,
        in_specs=(P(fsdp, seq, None), P(fsdp, None, seq, None), P(fsdp, None, None), rows, rows),
        out_specs=(P(fsdp, seq, None), rows, rows),
        check_vma=False,
    )
```

```python
import jax
import jax.numpy as jnp
import numpy as np
from jax import lax
from jax.experimental import pallas as pl
from jax.experimental.pallas import tpu as pltpu
from jax.sharding import Mesh, PartitionSpec as P

loss_scale = 256.0
eps_norm = 1e-06

AXES = ("zh", "x", "y", "zl", "c")
SIZES = (2, 4, 4, 4, 2)
D, PH, DT, TOK = 3584, 1024, 1536, 256
HH, HO = PH // 2, DT // 2
ROWS_IN, ROWS_OUT = 112, 32
PACK = 320
HID = HH + HO
bf16, f32 = jnp.bfloat16, jnp.float32
NT = (((1,), (1,)), ((), ()))
TN = (((0,), (0,)), ((), ()))


def permute(v, move):
    pairs = []
    for i in range(256):
        here = [int(a) for a in np.unravel_index(i, SIZES)]
        there = [a % s for a, s in zip(move(*here), SIZES)]
        pairs.append((i, int(np.ravel_multi_index(there, SIZES))))
    return lax.ppermute(v, AXES, pairs)


def first_axis(v, d):
    return permute(
        v, lambda zh, x, y, zl, c: (zh, x + d * (c == 0), y + d * (c == 1), zl, c)
    )


def second_axis(v, d):
    return permute(
        v, lambda zh, x, y, zl, c: (zh, x + d * (c == 1), y + d * (c == 0), zl, c)
    )


def swap_cores(v):
    return permute(v, lambda zh, x, y, zl, c: (zh, x, y, zl, 1 - c))


def place_of(core, x, y, d3, d2):
    sx = lax.rem(x + jnp.where(core == 0, d2, d3), 4)
    sy = lax.rem(y + jnp.where(core == 0, d3, d2), 4)
    return sx, sy


SHIFTS = (0, 1, 3, 2)
PIECES = ((0, 0, 512), (1, 0, 256), (3, 256, 256), (1, 256, 256), (3, 0, 256), (2, 0, 256), (2, 256, 256))


def head_kernel(place, latent, picked, *refs):
    own, oth = refs[0:7], refs[7:14]
    grad_pre_ref, keep_ref, give_ref, w_in_out = refs[14:18]
    w_in, w_out, pre, pred, gpred, sems = refs[18:]
    x, y, c = place[0], place[1], place[2]

    def fetch(pieces, core, top, sem):
        for ref, (d3, left, wide) in zip(pieces, PIECES):
            for j, d2 in enumerate(SHIFTS):
                sx, sy = place_of(core, x, y, 4 - d3, 4 - d2)
                b = sx * 4 + sy
                src = ref.at[j]

                def bring(first, rows, at, size, dst):
                    pltpu.make_async_copy(
                        src.at[pl.ds(first, rows), pl.ds(at, size)], dst, sems.at[sem]
                    ).start()

                def lane(first, size):
                    return pl.ds(pl.multiple_of(first, 256), size)

                if top:
                    bring(0, 224, 0, wide, w_in.at[b, :, lane(core * HH + left, wide)])
                else:
                    bring(
                        224, 64, 0, wide, w_out.at[b, :, lane(core * HO + left, wide)]
                    )
                    for at in range(0, wide, 256):
                        rows = pl.ds((left + at) // 8, 32)
                        dst = w_out.at[b, rows, lane(core * HO + 512, 256)]
                        bring(288, 32, at, 256, dst)

    fetch(own, c, True, 0)
    fetch(oth, 1 - c, True, 1)
    fetch(own, c, False, 2)
    fetch(oth, 1 - c, False, 2)
    token = lax.broadcasted_iota(jnp.int32, (TOK, TOK), 0)
    row = lax.broadcasted_iota(jnp.int32, (TOK, TOK), 1)
    want = (token // 4 % 32) * 8 + token // 128 * 4 + token % 4
    expand = jnp.where(row == want, 1.0, 0.0).astype(bf16)
    goal = jnp.dot(expand, picked[...], preferred_element_type=f32)
    norm_goal = jnp.sqrt(jnp.sum(goal * goal, axis=1, keepdims=True) + eps_norm)
    half = w_in.at[:, :, pl.ds(0, HH)]
    for core, sem in ((c, 0), (1 - c, 1)):
        pltpu.make_async_copy(half, half, sems.at[sem]).wait()
        for j in range(2):
            cols = pl.ds(pl.multiple_of(core * HH + j * 256, 256), 256)
            part = jnp.zeros((TOK, 256), f32)
            for zh in range(2):
                part += jnp.dot(
                    latent[:, zh * 1792 : (zh + 1) * 1792],
                    w_in[:, zh * ROWS_IN : (zh + 1) * ROWS_IN, cols].reshape(1792, 256),
                    preferred_element_type=f32,
                )
            pre[:, cols] = part
            keep_ref[:, pl.ds(pl.multiple_of(HID + core * HH + j * 256, 256), 256)] = (
                part * jax.nn.sigmoid(part)
            ).astype(bf16)
    save = pltpu.make_async_copy(w_in, w_in_out, sems.at[3])
    save.start()
    pltpu.make_async_copy(w_out, w_out, sems.at[2]).wait()
    for j in range(6):
        cols = slice(j * 256, (j + 1) * 256)
        part = jnp.zeros((TOK, 256), f32)
        for zh in range(2):
            part += jnp.dot(
                keep_ref[:, HID + zh * HH : HID + (zh + 1) * HH],
                w_out[:, zh * 32 : (zh + 1) * 32, cols].reshape(HH, 256),
                preferred_element_type=f32,
            )
        pred[:, cols] = part
    guess = pred[...]
    norm_pred = jnp.sqrt(jnp.sum(guess * guess, axis=1, keepdims=True) + eps_norm)
    cosv = jnp.sum(guess * goal, axis=1, keepdims=True) / (norm_pred * norm_goal)
    gpred[...] = (
        -loss_scale
        * (goal / (norm_pred * norm_goal) - cosv * guess / (norm_pred * norm_pred))
    ).astype(bf16)
    for j in range(4):
        cols = slice(j * 256, (j + 1) * 256)
        zh, b = j // 2, j % 2 * 8
        grad_hidden = lax.dot_general(
            gpred[...],
            w_out[b : b + 8, zh * 32 : (zh + 1) * 32, :].reshape(256, DT),
            NT,
            preferred_element_type=f32,
        )
        part = pre[:, cols]
        sig = jax.nn.sigmoid(part)
        grad_pre_ref[:, cols] = (
            grad_hidden * (sig * (1.0 + part * (1.0 - sig)))
        ).astype(bf16)
    for ref, core in ((keep_ref, c), (give_ref, 1 - c)):
        ref[:, :HH] = grad_pre_ref[:, pl.ds(pl.multiple_of(core * HH, HH), HH)]
        ref[:, HH:HID] = gpred[:, pl.ds(pl.multiple_of(core * HO, 256), HO)]
    give_ref[:, HID:] = keep_ref[:, HID:]
    save.wait()


def head(place, latent, picked, own, oth):
    vmem = pl.BlockSpec(memory_space=pltpu.VMEM)
    hbm = pl.BlockSpec(memory_space=pltpu.HBM)
    return pl.pallas_call(
        head_kernel,
        in_specs=[pl.BlockSpec(memory_space=pltpu.SMEM)] + [vmem] * 2 + [hbm] * 14,
        out_specs=[vmem, vmem, vmem, hbm],
        out_shape=[
            jax.ShapeDtypeStruct((TOK, PH), bf16),
            jax.ShapeDtypeStruct((TOK, HID + PH), bf16),
            jax.ShapeDtypeStruct((TOK, HID + PH), bf16),
            jax.ShapeDtypeStruct((16, 2 * ROWS_IN, PH), bf16),
        ],
        scratch_shapes=[
            pltpu.VMEM((16, 2 * ROWS_IN, PH), bf16),
            pltpu.VMEM((16, 2 * ROWS_OUT, DT), bf16),
            pltpu.VMEM((TOK, PH), f32),
            pltpu.VMEM((TOK, DT), f32),
            pltpu.VMEM((TOK, DT), bf16),
            pltpu.SemaphoreType.DMA((4,)),
        ],
        compiler_params=pltpu.CompilerParams(vmem_limit_bytes=48 * 2**20),
        cost_estimate=pl.CostEstimate(
            flops=5_000_000_000, bytes_accessed=30_000_000, transcendentals=600_000
        ),
        name="head",
    )(place, latent, picked, *own, *oth)


def tail_kernel(place, lat_a, lat_b, keep, rcv, *refs):
    outs = refs[:8]
    p_in, p_out = refs[8:]
    x, y, c = place[0], place[1], place[2]
    gpred = jnp.concatenate([keep[:, HH:HID], rcv[:, HH:HID]], axis=0)
    for zh in range(2):
        hid = slice(HID + zh * HH, HID + (zh + 1) * HH)
        hidden = jnp.concatenate([keep[:, hid], rcv[:, hid]], axis=0)
        p_out[zh * HH : (zh + 1) * HH] = lax.dot_general(
            hidden, gpred, TN, preferred_element_type=f32
        ).astype(bf16)
    for t in range(8):
        rows = slice(t * 448, (t + 1) * 448)
        p_in[rows] = (
            jnp.dot(lat_a[rows], keep[:, :HH], preferred_element_type=f32)
            + jnp.dot(lat_b[rows], rcv[:, :HH], preferred_element_type=f32)
        ).astype(bf16)
    for d3 in range(4):
        for d2 in range(4):
            sx, sy = place_of(c, x, y, d3, d2)
            b = sx * 4 + sy
            for zh in range(2):
                top = pl.ds(pl.multiple_of((zh * 16 + b) * ROWS_IN, 16), ROWS_IN)
                low = pl.ds(pl.multiple_of((zh * 16 + b) * ROWS_OUT, 32), ROWS_OUT)
                for h in range(2):
                    out = outs[d3 * 2 + h]
                    cols = slice(h * 256, (h + 1) * 256)
                    out[d2, zh * ROWS_IN : (zh + 1) * ROWS_IN] = p_in[top, cols]
                    out[d2, 224 + zh * 32 : 256 + zh * 32] = p_out[low, cols]
                outs[d3 * 2 + zh][d2, 288:320] = p_out[low, 512:768]


def tail(place, lat_a, lat_b, keep, rcv):
    vmem = pl.BlockSpec(memory_space=pltpu.VMEM)
    return pl.pallas_call(
        tail_kernel,
        in_specs=[pl.BlockSpec(memory_space=pltpu.SMEM)] + [vmem] * 4,
        out_specs=[vmem] * 8,
        out_shape=[jax.ShapeDtypeStruct((4, PACK, 256), bf16)] * 8,
        scratch_shapes=[pltpu.VMEM((D, HH), bf16), pltpu.VMEM((PH, HO), bf16)],
        compiler_params=pltpu.CompilerParams(vmem_limit_bytes=40 * 2**20),
        cost_estimate=pl.CostEstimate(
            flops=2_700_000_000, bytes_accessed=12_000_000, transcendentals=0
        ),
        name="tail",
    )(place, lat_a, lat_b, keep, rcv)


def back_kernel(grad_pre, w_in, out):
    out[...] = lax.dot_general(
        grad_pre[...], w_in[...].reshape(896, PH), NT, preferred_element_type=f32
    ).astype(bf16)


def back(grad_pre, w_in):
    return pl.pallas_call(
        back_kernel,
        grid=(4,),
        in_specs=[
            pl.BlockSpec((TOK, PH), lambda i: (0, 0)),
            pl.BlockSpec((8, ROWS_IN, PH), lambda i: (i % 2, i // 2, 0)),
        ],
        out_specs=pl.BlockSpec((TOK, 896), lambda i: (0, i)),
        out_shape=jax.ShapeDtypeStruct((TOK, D), bf16),
        compiler_params=pltpu.CompilerParams(vmem_limit_bytes=32 * 2**20),
        cost_estimate=pl.CostEstimate(
            flops=1_900_000_000, bytes_accessed=10_000_000, transcendentals=0
        ),
        name="back",
    )(grad_pre, w_in)


def add(*terms):
    return sum(t.astype(f32) for t in terms).astype(bf16)


def fan_kernel(top, low, out):
    for h in range(2):
        lows = low[:, h * HO : (h + 1) * HO].astype(f32)
        block = jnp.concatenate(
            [
                top[:, h * HH : (h + 1) * HH].astype(f32),
                lows[:, :512],
                jnp.concatenate([lows[0:2, 512:], lows[2:4, 512:]], axis=1),
            ],
            axis=0,
        ).astype(bf16)
        for z in range(8):
            out[z * 2 + h] = block


def fan_out(proj_in, proj_out):
    return pl.pallas_call(
        fan_kernel,
        out_shape=jax.ShapeDtypeStruct((16, 20, HH), bf16),
        name="fan_out",
    )(proj_in, proj_out)


def fan_in_kernel(last, top, low):
    for h in range(2):
        total = last[h].astype(f32)
        for z in range(1, 8):
            total += last[z * 2 + h].astype(f32)
        top[:, h * HH : (h + 1) * HH] = total[:14]
        low[:, h * HO : h * HO + 512] = total[14:18]
        low[0:2, h * HO + 512 : (h + 1) * HO] = total[18:20, :256]
        low[2:4, h * HO + 512 : (h + 1) * HO] = total[18:20, 256:]


def fan_in(last):
    return pl.pallas_call(
        fan_in_kernel,
        out_shape=[
            jax.ShapeDtypeStruct((14, PH), f32),
            jax.ShapeDtypeStruct((4, DT), f32),
        ],
        name="fan_in",
    )(last)


def per_device(latent, targets, index_map, proj_in, proj_out):
    x, y, c = lax.axis_index("x"), lax.axis_index("y"), lax.axis_index("c")
    place = jnp.stack([x, y, c]).astype(jnp.int32)

    column = lax.all_to_all(
        fan_out(proj_in, proj_out),
        ("zh", "zl", "c"), split_axis=0, concat_axis=0, tiled=True,
    )
    third = jnp.concatenate([column[:, 18:, :256], column[:, 18:, 256:]], axis=1)
    packed = jnp.concatenate(
        [
            column[:, :14].reshape(224, HH),
            column[:, 14:18].reshape(64, HH),
            third.reshape(2, 32, 256).transpose(1, 0, 2).reshape(32, HH),
        ],
        axis=0,
    )

    seq = lax.axis_index("zh") * 16 + x * 4 + y
    slab = targets[0].transpose(1, 0, 2)
    wide, tall = slab.shape[:2]
    cell = lax.dynamic_slice_in_dim(index_map[0], seq * 4, 4, 1)
    cell = (cell % (wide * 32) - seq * wide) * tall + cell // (wide * 32)
    pick = (
        cell.reshape(TOK)[:, None] == jnp.arange(wide * tall, dtype=jnp.int32)[None]
    ).astype(bf16)
    sent = jnp.dot(
        pick, slab.reshape(wide * tall, DT), preferred_element_type=f32
    ).astype(bf16).reshape(32, 8, DT)
    lat_t = latent[0].T
    packed, sent, lat_t = lax.optimization_barrier((packed, sent, lat_t))
    got = lax.all_to_all(
        sent, ("zh", "x", "y"), split_axis=0, concat_axis=0, tiled=True
    )
    picked = got.reshape(TOK, DT)
    line = jnp.stack([packed] + [first_axis(packed, d) for d in SHIFTS[1:]])
    lat_o = swap_cores(lat_t)
    left, right = lax.optimization_barrier((line[..., :256], line[..., 256:]))
    left1, right3 = second_axis(left, 1), second_axis(right, 3)
    right1, left3 = second_axis(right, 1), second_axis(left, 3)
    left2, right2 = second_axis(left1, 1), second_axis(right3, 3)
    right2, left2, picked = lax.optimization_barrier((right2, left2, picked))
    own = [line, left1, right3, right1, left3, left2, right2]
    oth = [swap_cores(v) for v in own]

    grad_pre, keep, give, w_in = head(place, latent[0], picked, own, oth)
    rcv = swap_cores(give)
    sums = tail(place, lat_t, lat_o, keep, rcv)
    lefts, rights = sums[0::2], sums[1::2]
    via_left, via_right = second_axis(lefts[2], 1), second_axis(rights[2], 3)
    rights1, lefts3 = second_axis(rights[1], 1), second_axis(lefts[3], 3)
    lefts1 = second_axis(add(lefts[1], via_left), 1)
    rights3 = second_axis(add(rights[3], via_right), 3)
    grad_latent = back(grad_pre, w_in)
    lefts1, grad_latent = lax.optimization_barrier((lefts1, grad_latent))
    line_sum = [
        jnp.concatenate(
            [
                add(lefts[0][k], lefts1[k], lefts3[k]),
                add(rights[0][k], rights1[k], rights3[k]),
            ],
            axis=1,
        )
        for k in range(4)
    ]
    got2 = [first_axis(line_sum[d], d) for d in SHIFTS[1:]]
    mine = add(line_sum[0], *got2)
    third = mine[288:].reshape(32, 2, 256).transpose(1, 0, 2).reshape(16, 4, 256)
    last = lax.all_to_all(
        jnp.concatenate(
            [
                mine[:224].reshape(16, 14, HH),
                mine[224:288].reshape(16, 4, HH),
                jnp.concatenate([third[:, :2], third[:, 2:]], axis=2),
            ],
            axis=1,
        ),
        ("zh", "zl", "c"), split_axis=0, concat_axis=0, tiled=True,
    )
    grad_in, grad_out = fan_in(last)
    return grad_latent[None], grad_in, grad_out


def solution(mesh):
    fine = Mesh(mesh.devices.reshape(SIZES), AXES)
    seq, fsdp = ("zh", "x", "y"), ("zl", "c")
    rows = P(AXES, None)
    return jax.shard_map(
        per_device,
        mesh=fine,
        in_specs=(P(fsdp, seq, None), P(fsdp, None, seq, None), P(fsdp, None, None), rows, rows),
        out_specs=(P(fsdp, seq, None), rows, rows),
        check_vma=False,
    )
```
